256 devices in a mesh: section: 8 (over y_lo, x), sc: 32 (over z, y_hi, core).
Axes of the slice: x: 4, y: 4 (y_hi: 2, y_lo: 2; y = y_hi * 2 + y_lo), z: 8, core: 2. Of those that a mesh axis runs over, the one named last changes fastest.
Arguments:
- observed_vector: float32 [4096, 14, 128], P('sc'), may hold values from -6 to 6
- propagation_matrix: float32 [4096, 16, 4, 128], P('sc', 'section'), may hold values from -0.5 to 0.5
- noise_var: float32 [4096], P('sc'), may hold values from 0.005 to 2.5, as said below
- sliced_constellation: int32 [4096, 14, 64], P('sc', None, 'section'), may hold values from 0 to 15
- detection_sequence: int32 [16], replicated, may hold values from 0 to 15, as said below
Outputs:
- estimates: float32 [4096, 14, 128], P('sc', None, 'section')
The draws below stay inside these ranges and needn't reach their ends.
Inputs may be any that keep to these rules, and one draw needn't show every extreme that they name: `noise_var`: positive variances. `detection_sequence`: a permutation taken in blocks of 2 positions: each block of positions holds the 2 group ids 2 * m to 2 * m + 1 of one m, in a rotated order; the first block of positions takes m = 4, the second m = 0.
All inputs are finite; a program needn't handle non-finite values.
Results may differ from the reference program's by a relative error of at most 0.0001.
Values sent between devices are 32-bit elements; how exact they have to be, the bound alone decides.
No kernel may reach another device: no remote copies, remote signals or barrier semaphores. Data moves between devices by JAX's collectives and lax.ppermute only.
A program may use at most 64 MiB of HBM per device.

```python
import jax
import jax.numpy as jnp
from jax import lax

SENSOR_ELEMENTS = 64
TERMINAL_COUNT = 4
OFDM_TIME_SLOTS = 14
GRP_DEV = 2
TONE_COUNT = 4096
CLUSTER_COUNT = 16


def draw_noise_var(key, part):
    sequence_index = jnp.arange(TONE_COUNT, dtype=jnp.float32) / TONE_COUNT
    base = 0.01 * jnp.exp(sequence_index * 4.605170186)
    multiplier = jnp.exp(jax.random.uniform(key, (TONE_COUNT,), jnp.float32, -0.35, 0.35))
    return base * multiplier


def force_entry(order, where_slot, wanted):
    present = order[where_slot]
    order = jnp.where(order == wanted, present, order)
    return order.at[where_slot].set(wanted)


def draw_detection_sequence(key, part):
    block_count = CLUSTER_COUNT // GRP_DEV
    order = jax.random.permutation(jax.random.fold_in(key, 11), block_count).astype(jnp.int32)
    order = force_entry(order, 0, block_count // 2)
    order = force_entry(order, 1, 0)
    offsets = jax.random.randint(jax.random.fold_in(key, 12), (block_count,), 0, GRP_DEV, dtype=jnp.int32)
    within = jnp.arange(GRP_DEV, dtype=jnp.int32)
    sequence = GRP_DEV * order[:, None] + (within[None, :] + offsets[:, None]) % GRP_DEV
    return sequence.reshape(-1).astype(jnp.int32)


def set_ends(values, rng, smallest, largest):
    longest = values.shape.index(max(values.shape))
    spots = []
    for shift in (0, 1):
        where = [jax.random.randint(jax.random.fold_in(rng, axis), (), 0, length) for axis, length in enumerate(values.shape)]
        where[longest] = (where[longest] + shift) % values.shape[longest]
        spots.append(tuple(where))
    return values.at[spots[0]].set(smallest).at[spots[1]].set(largest)


def shard_levels(rng, dims, cuts, least, largest):
    def one(axis_at, parts):
        steps = jax.random.uniform(jax.random.fold_in(jax.random.fold_in(rng, 6), axis_at), (parts,), jnp.float32, least / len(cuts), largest / len(cuts))
        return jnp.repeat(jnp.exp(steps), dims[axis_at] // parts).reshape((-1,) + (1,) * (len(dims) - axis_at - 1))

    factor_of = one(*cuts[0])
    for cut in cuts[1:]:
        factor_of = factor_of * one(*cut)
    return factor_of


def centred(rng, dims, scale, limit, shards=(), kind=jnp.bfloat16):
    drawn = scale * jax.random.normal(rng, dims, jnp.float32)
    if shards:
        drawn = drawn * shard_levels(rng, dims, shards, -0.22, 0.18)
    return jnp.clip(drawn, -limit, limit).astype(kind)


def setup_inputs(seed: int = 0) -> dict:
    arg_keys = jax.random.split(jax.random.key(seed), 6)
    observed_vector = centred(arg_keys[0], (TONE_COUNT, OFDM_TIME_SLOTS, 2 * SENSOR_ELEMENTS), 1.0, 6.0, ((0, 32),), jnp.float32)
    propagation_matrix = centred(arg_keys[1], (TONE_COUNT, CLUSTER_COUNT, TERMINAL_COUNT, 2 * SENSOR_ELEMENTS), (2 * SENSOR_ELEMENTS) ** -0.5, 0.5, ((0, 32), (1, 8)), jnp.float32)
    noise_var = draw_noise_var(jax.random.fold_in(arg_keys[5], 71), 0)
    sliced_constellation = set_ends(jax.random.randint(arg_keys[3], (TONE_COUNT, OFDM_TIME_SLOTS, CLUSTER_COUNT * TERMINAL_COUNT), 0, 16), jax.random.fold_in(arg_keys[3], 1), 0, 15).astype(jnp.int32)
    detection_sequence = draw_detection_sequence(jax.random.fold_in(arg_keys[5], 71), 0)
    return {"observed_vector": observed_vector, "propagation_matrix": propagation_matrix, "noise_var": noise_var, "sliced_constellation": sliced_constellation, "detection_sequence": detection_sequence}


ROOT_TEN = 3.1622776601683795

def rotate(vectors):
    half = vectors.shape[-1] // 2
    return jnp.concatenate([-vectors[..., half:], vectors[..., :half]], axis=-1)

def symbol_values(constellation_labels):
    real_part = (2 * (constellation_labels % 4) - 3).astype(jnp.float32) / ROOT_TEN
    imag_part = (2 * (constellation_labels // 4) - 3).astype(jnp.float32) / ROOT_TEN
    return jnp.concatenate([real_part, imag_part], axis=-1)

def invert_small(gram):
    width = gram.shape[-1]
    entry = [[gram[..., i, j] for j in range(width)] for i in range(width)]
    lower = [[None] * width for i in range(width)]
    for j in range(width):
        pivot = entry[j][j]
        for k in range(j):
            pivot = pivot - lower[j][k] * lower[j][k]
        lower[j][j] = jnp.sqrt(pivot)
        recip = 1.0 / lower[j][j]
        for i in range(j + 1, width):
            value = entry[i][j]
            for k in range(j):
                value = value - lower[i][k] * lower[j][k]
            lower[i][j] = value * recip
    inv_lower = [[None] * width for i in range(width)]
    for i in range(width):
        inv_lower[i][i] = 1.0 / lower[i][i]
        for j in range(i):
            value = lower[i][j] * inv_lower[j][j]
            for k in range(j + 1, i):
                value = value + lower[i][k] * inv_lower[k][j]
            inv_lower[i][j] = -value * inv_lower[i][i]
    rows = []
    for i in range(width):
        cols = []
        for j in range(width):
            start = max(i, j)
            value = inv_lower[start][i] * inv_lower[start][j]
            for k in range(start + 1, width):
                value = value + inv_lower[k][i] * inv_lower[k][j]
            cols.append(value)
        rows.append(jnp.stack(cols, axis=-1))
    return jnp.stack(rows, axis=-2)

def filters_of(basis, noise):
    width = basis.shape[-2]
    eye = jnp.eye(width, dtype=jnp.float32)
    gram = jnp.einsum('sik,sjk->sij', basis, basis, precision=lax.Precision.HIGHEST) + noise[:, None, None] * eye
    inverse = invert_small(gram)
    filt = jnp.einsum('sij,sjk->sik', inverse, basis, precision=lax.Precision.HIGHEST)
    diag = jnp.diagonal(inverse, axis1=1, axis2=2)[:, :width // 2]
    amplitude_level = 1.0 - noise[:, None] * diag
    return (filt, amplitude_level)

def reference(observed_vector, propagation_matrix, noise_var, sliced_constellation, detection_sequence):
    padded = jnp.pad(propagation_matrix, ((1, 1), (0, 0), (0, 0), (0, 0)))
    smooth = 0.5 * padded[1:-1] + 0.25 * (padded[:-2] + padded[2:])
    basis_all = jnp.concatenate([smooth, rotate(smooth)], axis=2)
    constellation_labels = jnp.take(sliced_constellation.reshape(TONE_COUNT, OFDM_TIME_SLOTS, CLUSTER_COUNT, TERMINAL_COUNT), detection_sequence.astype(jnp.int32), axis=2)
    symbols = symbol_values(constellation_labels)
    current = observed_vector
    results = []
    for slot in range(CLUSTER_COUNT):
        basis = basis_all[:, slot]
        filt, amplitude_level = filters_of(basis, noise_var)
        average_amplitude = lax.optimization_barrier(jnp.sum(amplitude_level, axis=0)) / TONE_COUNT
        scale = jnp.concatenate([average_amplitude, average_amplitude])
        est = jnp.einsum('sik,stk->sti', filt, current, precision=lax.Precision.HIGHEST) / scale
        results.append(est)
        remove_decided = jnp.einsum('sti,sik->stk', symbols[:, :, slot], basis, precision=lax.Precision.HIGHEST)
        current = current - remove_decided
    return jnp.concatenate(results, axis=2)
```

```python
import jax
import jax.numpy as jnp
from jax import lax
from jax.experimental import pallas as pl
from jax.experimental.pallas import tpu as pltpu
from jax.sharding import PartitionSpec as P

ROOT_TEN = 3.1622776601683795
F32 = jnp.float32
BF16 = jnp.bfloat16
VMEM = pl.BlockSpec(memory_space=pltpu.VMEM)
PARAMS = pltpu.CompilerParams(vmem_limit_bytes=32 * 1024 * 1024)


def hermitian_inverse(a, b, noise):
    n = 4
    zr = [[None] * n for _ in range(n)]
    zi = [[None] * n for _ in range(n)]
    for i in range(n):
        for j in range(i + 1):
            zr[i][j] = a[j, i] + noise if i == j else a[j, i]
            zi[i][j] = None if i == j else b[j, i]
    lr = [[None] * n for _ in range(n)]
    li = [[None] * n for _ in range(n)]
    recip = [None] * n
    for j in range(n):
        d = zr[j][j]
        for k in range(j):
            d = d - (zr[j][k] * lr[j][k] + zi[j][k] * li[j][k])
        recip[j] = 1.0 / d
        for i in range(j + 1, n):
            re, im = zr[i][j], zi[i][j]
            for k in range(j):
                re = re - (zr[i][k] * lr[j][k] + zi[i][k] * li[j][k])
                im = im - (zi[i][k] * lr[j][k] - zr[i][k] * li[j][k])
            zr[i][j], zi[i][j] = re, im
            lr[i][j], li[i][j] = re * recip[j], im * recip[j]
    mr = [[None] * n for _ in range(n)]
    mi = [[None] * n for _ in range(n)]
    for j in range(n):
        for i in range(j + 1, n):
            re, im = lr[i][j], li[i][j]
            for k in range(j + 1, i):
                re = re + (lr[i][k] * mr[k][j] - li[i][k] * mi[k][j])
                im = im + (lr[i][k] * mi[k][j] + li[i][k] * mr[k][j])
            mr[i][j], mi[i][j] = -re, -im
    p, q = {}, {}
    for i in range(n):
        for j in range(i, n):
            if i == j:
                re, im = recip[j], None
            else:
                re, im = mr[j][i] * recip[j], -(mi[j][i] * recip[j])
            for k in range(j + 1, n):
                sr, si = mr[k][j] * recip[k], mi[k][j] * recip[k]
                re = re + (mr[k][i] * sr + mi[k][i] * si)
                if i != j:
                    im = im + (mr[k][i] * si - mi[k][i] * sr)
            p[i, j] = re
            if i != j:
                q[i, j] = im
    return p, q


def gram_entries(t_ref):
    a, b = {}, {}
    for g in range(2):
        sa, sb = {}, {}
        for c in range(8):
            x = [t_ref[g * 4 + u, c * 8 : c * 8 + 8, :] for u in range(4)]
            y = [t_ref[g * 4 + u, 64 + c * 8 : 72 + c * 8, :] for u in range(4)]
            for u in range(4):
                for w in range(u, 4):
                    v = x[u] * x[w] + y[u] * y[w]
                    sa[u, w] = v if c == 0 else sa[u, w] + v
                    if w > u:
                        v = y[u] * x[w] - x[u] * y[w]
                        sb[u, w] = v if c == 0 else sb[u, w] + v
        for key in sa:
            a.setdefault(key, []).append(jnp.sum(sa[key], axis=0, keepdims=True))
        for key in sb:
            b.setdefault(key, []).append(jnp.sum(sb[key], axis=0, keepdims=True))
    a = {key: jnp.concatenate(a[key], axis=0) for key in a}
    b = {key: jnp.concatenate(b[key], axis=0) for key in b}
    return a, b


def smooth_kernel(h_ref, before_ref, after_ref, labels_ref, x_ref):
    rows = 128
    for f in range(rows):
        left = before_ref[0] if f == 0 else h_ref[f - 1]
        right = after_ref[0] if f == rows - 1 else h_ref[f + 1]
        m, at = divmod(f, 16)
        x_ref[m, at * 8 : at * 8 + 8, :] = 0.5 * h_ref[f] + 0.25 * (left + right)
    labels = labels_ref[...].astype(F32)
    labels = jnp.concatenate([labels, jnp.zeros((16, 128), F32)], axis=0).T
    for m in range(8):
        x_ref[m, 128:144, :] = labels[m * 16 : m * 16 + 16, :]


def gain_kernel(x_ref, noise_ref, out_ref, t_ref):
    for i in range(8):
        rows = [x_ref[m, pl.ds(i, 16, stride=8), :] for m in range(8)]
        t_ref[i] = jnp.concatenate(rows, axis=0).T
    a, b = gram_entries(t_ref)
    noise = noise_ref[...]
    p, _ = hermitian_inverse(a, b, noise)
    out_ref[...] = jnp.concatenate([1.0 - noise * p[u, u] for u in range(4)], axis=0)


def detect_kernel(seq_ref, x_ref, y_ref, noise_ref, out_ref, ys_ref, yf_ref, v_ref, t_ref, f_ref, s_ref, e_ref, sem):
    me = lax.axis_index("section")
    first = pl.multiple_of(me * 16, 16)
    copy = pltpu.make_async_copy(y_ref.at[:, pl.ds(first, 16), :], ys_ref.at[pl.ds(0, 14)], sem)
    copy.start()
    ys_ref[14:16] = jnp.zeros((2, 16, 128), F32)

    for i in range(8):
        for f in range(16):
            v_ref[i, f * 8 : f * 8 + 8, :] = x_ref[pl.ds(f * 8 + i, 8, stride=144), :]
    for i in range(8):
        t_ref[i] = v_ref[i].T
    a, b = gram_entries(t_ref)
    column = jnp.broadcast_to(noise_ref[...], (128, 128)).T
    sub = lax.broadcasted_iota(jnp.int32, (128, 128), 0)
    lane = lax.broadcasted_iota(jnp.int32, (128, 128), 1)
    noise = jnp.sum(jnp.where(sub == first + lane // 8, column, 0.0), axis=0, keepdims=True)
    p, q = hermitian_inverse(a, b, noise)

    for g in range(2):
        pb = {key: jnp.broadcast_to(p[key][g : g + 1], (8, 128)) for key in p}
        qb = {key: jnp.broadcast_to(q[key][g : g + 1], (8, 128)) for key in q}
        for c in range(8):
            x = [t_ref[g * 4 + u, c * 8 : c * 8 + 8, :] for u in range(4)]
            y = [t_ref[g * 4 + u, 64 + c * 8 : 72 + c * 8, :] for u in range(4)]
            for u in range(4):
                fx = pb[u, u] * x[u]
                fy = pb[u, u] * y[u]
                for w in range(4):
                    if w != u:
                        key = (min(u, w), max(u, w))
                        fx = fx + pb[key] * x[w]
                        fy = fy + pb[key] * y[w]
                        if u < w:
                            fx = fx + qb[key] * y[w]
                            fy = fy - qb[key] * x[w]
                        else:
                            fx = fx - qb[key] * y[w]
                            fy = fy + qb[key] * x[w]
                f_ref[g * 4 + u, c * 8 : c * 8 + 8, :] = fx
                f_ref[g * 4 + u, 64 + c * 8 : 72 + c * 8, :] = fy
    for i in range(8):
        t_ref[i] = f_ref[i].T

    lane_row = lax.broadcasted_iota(jnp.int32, (1, 128), 1)
    lane_s, lane_u, lane_g = lane_row % 8, (lane_row // 8) % 4, (lane_row // 32) % 2
    wanted = jnp.zeros((1, 128), jnp.int32)
    for pos in range(16):
        wanted = jnp.where(lane_s * 2 + lane_g == pos, seq_ref[pos], wanted)
    row_u, row_g = sub % 4, (sub // 4) % 2
    own = lane[:16] // 8 == lax.broadcasted_iota(jnp.int32, (16, 128), 0)
    total = jnp.zeros((256, 128), F32)
    for m in range(8):
        pick = jnp.where((wanted == 2 * m + row_g) & (lane_u == row_u), 1.0, 0.0).astype(BF16)
        rows = []
        for f in range(16):
            at = m * 144 + 128 + f
            row = jnp.broadcast_to(x_ref[at : at + 1, :], (16, 128))
            rows.append(jnp.where(own, row, 0.0).astype(BF16))
        total = total + jnp.dot(jnp.concatenate(rows, axis=0), pick, preferred_element_type=F32)
    upper = jnp.floor(total * 0.25)
    re = 2.0 * (total - 4.0 * upper) - 3.0
    im = 2.0 * upper - 3.0
    for f in range(16):
        s_ref[f * 32 : f * 32 + 16, :] = re[f * 16 : f * 16 + 16]
        s_ref[f * 32 + 16 : f * 32 + 32, :] = im[f * 16 : f * 16 + 16]

    row = lax.broadcasted_iota(jnp.int32, (64, 128), 0)
    col = lax.broadcasted_iota(jnp.int32, (64, 128), 1)
    earlier = 2 * (row % 8) + row // 32 < 2 * (col % 8) + (col // 32) % 2
    sign = jnp.where(lane_row < 64, -1.0, 1.0)
    copy.wait()
    yf_ref[...] = ys_ref[...].reshape(256, 128)
    nt = (((1,), (1,)), ((), ()))
    for f in range(16):
        at = slice(f * 8, f * 8 + 8)
        filt = jnp.concatenate([t_ref[i, at, :] for i in range(8)], axis=0)
        filt = jnp.concatenate([filt, pltpu.roll(filt, 64, 1) * sign], axis=0)
        fh = filt.astype(BF16)
        fl = (filt - fh.astype(F32)).astype(BF16)
        left = jnp.concatenate([v_ref[i, at, :] for i in range(8)] + [yf_ref[pl.ds(f, 16, stride=16), :]], axis=0)
        lh = left.astype(BF16)
        ll = (left - lh.astype(F32)).astype(BF16)
        xz = lax.dot_general(lh, fh, nt, preferred_element_type=F32)
        xz = xz + lax.dot_general(lh, fl, nt, preferred_element_type=F32)
        xz = xz + lax.dot_general(ll, fh, nt, preferred_element_type=F32)
        cross = jnp.where(earlier, xz[:64], 0.0)
        ch = cross.astype(BF16)
        cl = (cross - ch.astype(F32)).astype(BF16)
        sym = s_ref[f * 32 : f * 32 + 32, :64].astype(BF16)
        gone = jnp.dot(sym, ch, preferred_element_type=F32) + jnp.dot(sym, cl, preferred_element_type=F32)
        gone = gone[:16] + pltpu.roll(gone[16:], 64, 1) * sign
        e_ref[pl.ds(f, 16, stride=16), :] = xz[64:] - gone * (1.0 / ROOT_TEN)

    for half in range(2):
        turned = e_ref[half * 128 : half * 128 + 128, :].T
        for c in range(2):
            for g in range(2):
                for u in range(4):
                    at = (c * 8 + g * 4 + u) * 8
                    out_ref[pl.ds(half * 16 + g * 8 + c * 4 + u, 8, stride=32), :] = turned[at : at + 8, :]


def finish_kernel(count, est_ref, gain_ref, out_ref):
    total = jnp.sum(gain_ref[...], axis=1, keepdims=True)
    recip = count / total
    block = lax.broadcasted_iota(jnp.int32, (8, 128), 1) // 16
    for g in range(2):
        users = [recip[u * 2 + g : u * 2 + g + 1] for u in range(4)]
        scale = jnp.broadcast_to(jnp.concatenate(users + users, axis=0), (8, 128))
        for half in range(2):
            x = [est_ref[m, half, g * 8 : g * 8 + 8, :] for m in range(8)]
            for bit in (1, 2, 4):
                low = (block & bit) == 0
                new = list(x)
                for i in range(8):
                    if i & bit == 0:
                        j = i | bit
                        new[i] = jnp.where(low, x[i], pltpu.roll(x[j], 16 * bit, 1))
                        new[j] = jnp.where(low, pltpu.roll(x[i], 128 - 16 * bit, 1), x[j])
                x = new
            for i in range(8):
                t = half * 8 + i
                if t < 14:
                    out_ref[t, g * 8 : g * 8 + 8, :] = x[i] * scale


def halo(h):
    size = lax.axis_size("sc")
    up = [(i, i + 1) for i in range(size - 1)]
    down = [(j, i) for i, j in up]
    return lax.ppermute(h[-1:], "sc", up), lax.ppermute(h[:1], "sc", down)


def over_sections(x):
    return lax.all_to_all(x, "section", split_axis=0, concat_axis=0, tiled=True)


def over_subcarriers(x):
    size = lax.axis_size("sc")
    bit = 1
    while bit < size:
        x = x + lax.ppermute(x, "sc", [(i, i ^ bit) for i in range(size)])
        bit *= 2
    return x


def local(observed_vector, propagation_matrix, noise_var, sliced_constellation, detection_sequence):
    h = propagation_matrix.reshape(128, 8, 128)
    noise = noise_var.reshape(1, 128)
    labels = sliced_constellation.transpose(1, 2, 0).reshape(112, 128)
    y = observed_vector.transpose(1, 0, 2)
    before, after = halo(h)
    smooth = pl.pallas_call(
        smooth_kernel,
        out_shape=jax.ShapeDtypeStruct((8, 144, 128), F32),
        in_specs=[VMEM] * 4,
        out_specs=VMEM,
        compiler_params=PARAMS,
        name="smooth",
    )(h, before, after, labels)
    gathered = over_sections(smooth)
    gain = pl.pallas_call(
        gain_kernel,
        out_shape=jax.ShapeDtypeStruct((8, 128), F32),
        in_specs=[VMEM] * 2,
        out_specs=VMEM,
        scratch_shapes=[pltpu.VMEM((8, 128, 128), F32)],
        compiler_params=PARAMS,
        name="gain",
    )(smooth, noise)
    gain = over_subcarriers(gain)
    estimates = pl.pallas_call(
        detect_kernel,
        out_shape=jax.ShapeDtypeStruct((256, 128), F32),
        in_specs=[pl.BlockSpec(memory_space=pltpu.SMEM), VMEM, pl.BlockSpec(memory_space=pl.ANY), VMEM],
        out_specs=VMEM,
        scratch_shapes=[
            pltpu.VMEM((16, 16, 128), F32),
            pltpu.VMEM((256, 128), F32),
            pltpu.VMEM((8, 128, 128), F32),
            pltpu.VMEM((8, 128, 128), F32),
            pltpu.VMEM((8, 128, 128), F32),
            pltpu.VMEM((512, 128), F32),
            pltpu.VMEM((256, 128), F32),
            pltpu.SemaphoreType.DMA,
        ],
        compiler_params=PARAMS,
        name="detect",
    )(detection_sequence, gathered.reshape(1152, 128), y, noise)
    estimates = over_sections(estimates.reshape(8, 2, 16, 128))
    count = float(128 * lax.axis_size("sc"))
    out = pl.pallas_call(
        lambda *refs: finish_kernel(count, *refs),
        out_shape=jax.ShapeDtypeStruct((14, 16, 128), F32),
        in_specs=[VMEM] * 2,
        out_specs=VMEM,
        compiler_params=PARAMS,
        name="finish",
    )(estimates, gain)
    return out.transpose(2, 0, 1)


def solution(mesh):
    in_specs = (
        P("sc", None, None),
        P("sc", "section", None, None),
        P("sc"),
        P("sc", None, "section"),
        P(),
    )
    out_specs = P("sc", None, "section")
    return jax.shard_map(local, mesh=mesh, in_specs=in_specs, out_specs=out_specs, check_vma=False)
```

```python
import jax
import jax.numpy as jnp
from jax import lax
from jax.experimental import pallas as pl
from jax.experimental.pallas import tpu as pltpu
from jax.sharding import PartitionSpec as P

ROOT_TEN = 3.1622776601683795
F32 = jnp.float32
BF16 = jnp.bfloat16
VMEM = pl.BlockSpec(memory_space=pltpu.VMEM)
ANY = pl.BlockSpec(memory_space=pl.ANY)
PARAMS = pltpu.CompilerParams(vmem_limit_bytes=32 * 1024 * 1024)


def hermitian_inverse(a, b, noise):
    n = 4
    zr = [[None] * n for _ in range(n)]
    zi = [[None] * n for _ in range(n)]
    for i in range(n):
        for j in range(i + 1):
            zr[i][j] = a[j, i] + noise if i == j else a[j, i]
            zi[i][j] = None if i == j else b[j, i]
    lr = [[None] * n for _ in range(n)]
    li = [[None] * n for _ in range(n)]
    recip = [None] * n
    for j in range(n):
        d = zr[j][j]
        for k in range(j):
            d = d - (zr[j][k] * lr[j][k] + zi[j][k] * li[j][k])
        recip[j] = 1.0 / d
        for i in range(j + 1, n):
            re, im = zr[i][j], zi[i][j]
            for k in range(j):
                re = re - (zr[i][k] * lr[j][k] + zi[i][k] * li[j][k])
                im = im - (zi[i][k] * lr[j][k] - zr[i][k] * li[j][k])
            zr[i][j], zi[i][j] = re, im
            lr[i][j], li[i][j] = re * recip[j], im * recip[j]
    mr = [[None] * n for _ in range(n)]
    mi = [[None] * n for _ in range(n)]
    for j in range(n):
        for i in range(j + 1, n):
            re, im = lr[i][j], li[i][j]
            for k in range(j + 1, i):
                re = re + (lr[i][k] * mr[k][j] - li[i][k] * mi[k][j])
                im = im + (lr[i][k] * mi[k][j] + li[i][k] * mr[k][j])
            mr[i][j], mi[i][j] = -re, -im
    p, q = {}, {}
    for i in range(n):
        for j in range(i, n):
            if i == j:
                re, im = recip[j], None
            else:
                re, im = mr[j][i] * recip[j], -(mi[j][i] * recip[j])
            for k in range(j + 1, n):
                sr, si = mr[k][j] * recip[k], mi[k][j] * recip[k]
                re = re + (mr[k][i] * sr + mi[k][i] * si)
                if i != j:
                    im = im + (mr[k][i] * si - mi[k][i] * sr)
            p[i, j] = re
            if i != j:
                q[i, j] = im
    return p, q


def gram_entries(t_ref):
    a, b = {}, {}
    for g in range(2):
        sa, sb = {}, {}
        for c in range(8):
            x = [t_ref[g * 4 + u, c * 8 : c * 8 + 8, :] for u in range(4)]
            y = [t_ref[g * 4 + u, 64 + c * 8 : 72 + c * 8, :] for u in range(4)]
            for u in range(4):
                for w in range(u, 4):
                    v = x[u] * x[w] + y[u] * y[w]
                    sa[u, w] = v if c == 0 else sa[u, w] + v
                    if w > u:
                        v = y[u] * x[w] - x[u] * y[w]
                        sb[u, w] = v if c == 0 else sb[u, w] + v
        for key in sa:
            a.setdefault(key, []).append(jnp.sum(sa[key], axis=0, keepdims=True))
        for key in sb:
            b.setdefault(key, []).append(jnp.sum(sb[key], axis=0, keepdims=True))
    a = {key: jnp.concatenate(a[key], axis=0) for key in a}
    b = {key: jnp.concatenate(b[key], axis=0) for key in b}
    return a, b


def inner_kernel(seq_ref, h_ref, labels_ref, noise_ref, x_ref, aux_ref):
    for f in range(128):
        m, at = divmod(f, 16)
        if 0 < f < 127:
            x_ref[m, at * 8 : at * 8 + 8, :] = 0.5 * h_ref[f] + 0.25 * (h_ref[f - 1] + h_ref[f + 1])
        else:
            near = h_ref[1] if f == 0 else h_ref[126]
            x_ref[m, at * 8 : at * 8 + 8, :] = 0.5 * h_ref[f] + 0.25 * near
    labels = labels_ref[...].astype(F32)
    labels = jnp.concatenate([labels, jnp.zeros((16, 128), F32)], axis=0).T
    for m in range(8):
        x_ref[m, 128:144, :] = labels[m * 16 : m * 16 + 16, :]
    noise = noise_ref[...]
    column = jnp.broadcast_to(noise, (128, 128)).T
    sub = lax.broadcasted_iota(jnp.int32, (128, 128), 0)
    lane = lax.broadcasted_iota(jnp.int32, (128, 128), 1)
    first = lax.axis_index("section") * 16
    spread = jnp.sum(jnp.where(sub == first + lane // 8, column, 0.0), axis=0, keepdims=True)
    position = 2 * (lane[:1] % 8) + (lane[:1] // 32) % 2
    wanted = jnp.zeros((1, 128), jnp.int32)
    for pos in range(16):
        wanted = jnp.where(position == pos, seq_ref[pos], wanted)
    aux_ref[...] = jnp.concatenate([noise, spread, wanted.astype(F32), jnp.zeros((5, 128), F32)], axis=0)


def edge_kernel(x_ref, close_ref, far_ref, out_ref):
    even = lax.axis_index("sc") % 2 == 0
    close, far = close_ref[0], far_ref[0]
    out_ref[...] = x_ref[...]
    out_ref[0, 0:8, :] = x_ref[0, 0:8, :] + 0.25 * jnp.where(even, far, close)
    out_ref[7, 120:128, :] = x_ref[7, 120:128, :] + 0.25 * jnp.where(even, close, far)


def add_kernel(x_ref, other_ref, order_ref, out_ref):
    out_ref[...] = x_ref[...] + other_ref[...]


def gain_kernel(x_ref, close_ref, far_ref, aux_ref, out_ref, t_ref):
    even = lax.axis_index("sc") % 2 == 0
    close, far = close_ref[0], far_ref[0]
    before = 0.25 * jnp.where(even, far, close)
    after = 0.25 * jnp.where(even, close, far)
    row = lax.broadcasted_iota(jnp.int32, (16, 128), 0)
    for i in range(8):
        rows = [x_ref[m, pl.ds(i, 16, stride=8), :] for m in range(8)]
        rows[0] = rows[0] + jnp.where(row == 0, before[i : i + 1], 0.0)
        rows[7] = rows[7] + jnp.where(row == 15, after[i : i + 1], 0.0)
        t_ref[i] = jnp.concatenate(rows, axis=0).T
    a, b = gram_entries(t_ref)
    noise = aux_ref[0:1]
    p, _ = hermitian_inverse(a, b, noise)
    out_ref[...] = jnp.concatenate([1.0 - noise * p[u, u] for u in range(4)], axis=0)


def filter_kernel(x_ref, aux_ref, order_ref, v_ref, w_ref, s_ref, t_ref, f_ref):
    for i in range(8):
        for f in range(16):
            v_ref[i, f * 8 : f * 8 + 8, :] = x_ref[pl.ds(f * 8 + i, 8, stride=144), :]
    for i in range(8):
        t_ref[i] = v_ref[i].T
    a, b = gram_entries(t_ref)
    p, q = hermitian_inverse(a, b, aux_ref[1:2])

    for g in range(2):
        pb = {key: jnp.broadcast_to(p[key][g : g + 1], (8, 128)) for key in p}
        qb = {key: jnp.broadcast_to(q[key][g : g + 1], (8, 128)) for key in q}
        for c in range(8):
            x = [t_ref[g * 4 + u, c * 8 : c * 8 + 8, :] for u in range(4)]
            y = [t_ref[g * 4 + u, 64 + c * 8 : 72 + c * 8, :] for u in range(4)]
            for u in range(4):
                fx = pb[u, u] * x[u]
                fy = pb[u, u] * y[u]
                for w in range(4):
                    if w != u:
                        key = (min(u, w), max(u, w))
                        fx = fx + pb[key] * x[w]
                        fy = fy + pb[key] * y[w]
                        if u < w:
                            fx = fx + qb[key] * y[w]
                            fy = fy - qb[key] * x[w]
                        else:
                            fx = fx - qb[key] * y[w]
                            fy = fy + qb[key] * x[w]
                f_ref[g * 4 + u, c * 8 : c * 8 + 8, :] = fx
                f_ref[g * 4 + u, 64 + c * 8 : 72 + c * 8, :] = fy
    for i in range(8):
        w_ref[i] = f_ref[i].T

    sub = lax.broadcasted_iota(jnp.int32, (128, 128), 0)
    lane = lax.broadcasted_iota(jnp.int32, (128, 128), 1)
    lane_u = (lane[:1] // 8) % 4
    wanted = aux_ref[2:3].astype(jnp.int32)
    row_u, row_g = sub % 4, (sub // 4) % 2
    own = lane[:16] // 8 == lax.broadcasted_iota(jnp.int32, (16, 128), 0)
    total = jnp.zeros((256, 128), F32)
    for m in range(8):
        pick = jnp.where((wanted == 2 * m + row_g) & (lane_u == row_u), 1.0, 0.0).astype(BF16)
        rows = []
        for f in range(16):
            at = m * 144 + 128 + f
            row = jnp.broadcast_to(x_ref[at : at + 1, :], (16, 128))
            rows.append(jnp.where(own, row, 0.0).astype(BF16))
        total = total + jnp.dot(jnp.concatenate(rows, axis=0), pick, preferred_element_type=F32)
    upper = jnp.floor(total * 0.25)
    re = 2.0 * (total - 4.0 * upper) - 3.0
    im = 2.0 * upper - 3.0
    for f in range(16):
        s_ref[f * 32 : f * 32 + 16, :] = re[f * 16 : f * 16 + 16]
        s_ref[f * 32 + 16 : f * 32 + 32, :] = im[f * 16 : f * 16 + 16]


def cancel_kernel(half, v_ref, w_ref, s_ref, y_ref, order_ref, out_ref, ys_ref, yf_ref, e_ref, sem):
    start = half * 8
    first = pl.multiple_of(lax.axis_index("section") * 16 + start, 8)
    copy = pltpu.make_async_copy(y_ref.at[:, pl.ds(first, 8), :], ys_ref.at[pl.ds(0, 14)], sem)
    copy.start()
    ys_ref[14:16] = jnp.zeros((2, 8, 128), F32)
    row = lax.broadcasted_iota(jnp.int32, (64, 128), 0)
    col = lax.broadcasted_iota(jnp.int32, (64, 128), 1)
    earlier = 2 * (row % 8) + row // 32 < 2 * (col % 8) + (col // 32) % 2
    sign = jnp.where(col[:1] < 64, -1.0, 1.0)
    copy.wait()
    yf_ref[...] = ys_ref[...].reshape(128, 128)
    nt = (((1,), (1,)), ((), ()))
    for f in range(8):
        at = slice((start + f) * 8, (start + f) * 8 + 8)
        filt = jnp.concatenate([w_ref[i, at, :] for i in range(8)], axis=0)
        filt = jnp.concatenate([filt, pltpu.roll(filt, 64, 1) * sign], axis=0)
        fh = filt.astype(BF16)
        fl = (filt - fh.astype(F32)).astype(BF16)
        left = jnp.concatenate([v_ref[i, at, :] for i in range(8)] + [yf_ref[pl.ds(f, 16, stride=8), :]], axis=0)
        lh = left.astype(BF16)
        ll = (left - lh.astype(F32)).astype(BF16)
        xz = lax.dot_general(lh, fh, nt, preferred_element_type=F32)
        xz = xz + lax.dot_general(lh, fl, nt, preferred_element_type=F32)
        xz = xz + lax.dot_general(ll, fh, nt, preferred_element_type=F32)
        cross = jnp.where(earlier, xz[:64], 0.0)
        ch = cross.astype(BF16)
        cl = (cross - ch.astype(F32)).astype(BF16)
        sym = s_ref[(start + f) * 32 : (start + f) * 32 + 32, :64].astype(BF16)
        gone = jnp.dot(sym, ch, preferred_element_type=F32) + jnp.dot(sym, cl, preferred_element_type=F32)
        gone = gone[:16] + pltpu.roll(gone[16:], 64, 1) * sign
        e_ref[pl.ds(f, 16, stride=8), :] = xz[64:] - gone * (1.0 / ROOT_TEN)
    turned = e_ref[...].T
    for c in range(2):
        for g in range(2):
            for u in range(4):
                at = (c * 8 + g * 4 + u) * 8
                out_ref[pl.ds(g * 8 + c * 4 + u, 8, stride=16), :] = turned[at : at + 8, :]


def pack_kernel(one_ref, two_ref, order_ref, out_ref):
    for m in range(8):
        out_ref[m, 0] = one_ref[m * 16 : m * 16 + 16, :]
        out_ref[m, 1] = two_ref[m * 16 : m * 16 + 16, :]


def finish_kernel(count, est_ref, gain_ref, out_ref):
    total = jnp.sum(gain_ref[...], axis=1, keepdims=True)
    recip = count / total
    block = lax.broadcasted_iota(jnp.int32, (8, 128), 1) // 8
    for g in range(2):
        users = [recip[u * 2 + g : u * 2 + g + 1] for u in range(4)]
        scale = jnp.broadcast_to(jnp.concatenate(users + users, axis=0), (8, 128))
        x = [est_ref[i // 2, i % 2, g * 8 : g * 8 + 8, :] for i in range(16)]
        for bit in (1, 2, 4, 8):
            low = (block & bit) == 0
            new = list(x)
            for i in range(16):
                if i & bit == 0:
                    j = i | bit
                    new[i] = jnp.where(low, x[i], pltpu.roll(x[j], 8 * bit, 1))
                    new[j] = jnp.where(low, pltpu.roll(x[i], 128 - 8 * bit, 1), x[j])
            x = new
        for t in range(14):
            out_ref[t, g * 8 : g * 8 + 8, :] = x[t] * scale


def halo(h):
    size = lax.axis_size("sc")
    even = lax.axis_index("sc") % 2 == 0
    close = [(i, i ^ 1) for i in range(size)]
    far = [(i, i + 1) for i in range(1, size - 1, 2)]
    far = far + [(j, i) for i, j in far]
    far = lax.ppermute(jnp.where(even, h[:1], h[-1:]), "sc", far)
    close = lax.ppermute(jnp.where(even, h[-1:], h[:1]), "sc", close)
    return close, far


def over_sections(x):
    return lax.all_to_all(x, "section", split_axis=0, concat_axis=0, tiled=True)


def from_partner(x, bit):
    return lax.ppermute(x, "sc", [(i, i ^ bit) for i in range(lax.axis_size("sc"))])


def kernel(body, shape, in_specs, name, scratch=(), aliases=None, flops=0, moved=0):
    out = [jax.ShapeDtypeStruct(s, F32) for s in shape] if isinstance(shape, list) else jax.ShapeDtypeStruct(shape, F32)
    return pl.pallas_call(
        body,
        out_shape=out,
        in_specs=in_specs,
        out_specs=[VMEM] * len(shape) if isinstance(shape, list) else VMEM,
        scratch_shapes=list(scratch),
        input_output_aliases=aliases or {},
        compiler_params=PARAMS,
        cost_estimate=pl.CostEstimate(flops=flops, bytes_accessed=moved, transcendentals=0),
        name=name,
    )


def local(observed_vector, propagation_matrix, noise_var, sliced_constellation, detection_sequence):
    h = propagation_matrix.reshape(128, 8, 128)
    noise = noise_var.reshape(1, 128)
    labels = sliced_constellation.transpose(1, 2, 0).reshape(112, 128)
    y = observed_vector.transpose(1, 0, 2)
    big = (8, 128, 128)
    smem = pl.BlockSpec(memory_space=pltpu.SMEM)
    close, far = halo(h)
    inner, aux = kernel(inner_kernel, [(8, 144, 128), (8, 128)], [smem] + [VMEM] * 3, "inner", flops=10**6, moved=2 * 10**6)(
        detection_sequence, h, labels, noise
    )
    smooth = kernel(edge_kernel, (8, 144, 128), [VMEM] * 3, "edge")(inner, close, far)
    gathered = over_sections(smooth)
    gain = kernel(gain_kernel, (8, 128), [VMEM] * 4, "gain", [pltpu.VMEM(big, F32)], flops=10**6, moved=10**6)(inner, close, far, aux)

    def add(name, x, other, after):
        return kernel(add_kernel, (8, 128), [VMEM, VMEM, ANY], name)(x, other, after)

    def cancel(half, *args):
        scratch = [pltpu.VMEM((16, 8, 128), F32), pltpu.VMEM((128, 128), F32), pltpu.VMEM((128, 128), F32), pltpu.SemaphoreType.DMA]
        body = lambda *refs: cancel_kernel(half, *refs)
        specs = [VMEM, VMEM, VMEM, ANY, ANY]
        return kernel(body, (128, 128), specs, "cancel", scratch, flops=10**8, moved=4 * 10**6)(*args)

    gain = gain + from_partner(gain, 16)
    gain = add("add_a", gain, from_partner(gain, 1), gathered)
    tiles, filters, symbols = kernel(
        filter_kernel,
        [big, big, (512, 128)],
        [VMEM, VMEM, ANY],
        "filters",
        [pltpu.VMEM(big, F32), pltpu.VMEM(big, F32)],
        flops=10**8,
        moved=4 * 10**6,
    )(gathered.reshape(1152, 128), aux, gain)
    one = cancel(0, tiles, filters, symbols, y, gain)
    gain = add("add_b", gain, from_partner(gain, 2), one)
    two = cancel(1, tiles, filters, symbols, y, gain)
    gain = add("add_c", gain, from_partner(gain, 8), two)
    estimates = kernel(pack_kernel, (8, 2, 16, 128), [VMEM, VMEM, ANY], "pack")(one, two, gain)
    estimates = over_sections(estimates)
    gain = gain + from_partner(gain, 4)
    count = float(128 * lax.axis_size("sc"))
    body = lambda *refs: finish_kernel(count, *refs)
    out = kernel(body, (14, 16, 128), [VMEM] * 2, "finish")(estimates, gain)
    return out.transpose(2, 0, 1)


def solution(mesh):
    in_specs = (
        P("sc", None, None),
        P("sc", "section", None, None),
        P("sc"),
        P("sc", None, "section"),
        P(),
    )
    out_specs = P("sc", None, "section")
    return jax.shard_map(local, mesh=mesh, in_specs=in_specs, out_specs=out_specs, check_vma=False)
```

```python
import jax
import jax.numpy as jnp
from jax import lax
from jax.experimental import pallas as pl
from jax.experimental.pallas import tpu as pltpu
from jax.sharding import PartitionSpec as P

ROOT_TEN = 3.1622776601683795
F32 = jnp.float32
BF16 = jnp.bfloat16
VMEM = pl.BlockSpec(memory_space=pltpu.VMEM)
ANY = pl.BlockSpec(memory_space=pl.ANY)
SMEM = pl.BlockSpec(memory_space=pltpu.SMEM)
PARAMS = pltpu.CompilerParams(vmem_limit_bytes=32 * 1024 * 1024)


def hermitian_inverse(a, b, noise):
    n = 4
    zr = [[None] * n for _ in range(n)]
    zi = [[None] * n for _ in range(n)]
    for i in range(n):
        for j in range(i + 1):
            zr[i][j] = a[j, i] + noise if i == j else a[j, i]
            zi[i][j] = None if i == j else b[j, i]
    lr = [[None] * n for _ in range(n)]
    li = [[None] * n for _ in range(n)]
    recip = [None] * n
    for j in range(n):
        d = zr[j][j]
        for k in range(j):
            d = d - (zr[j][k] * lr[j][k] + zi[j][k] * li[j][k])
        recip[j] = 1.0 / d
        for i in range(j + 1, n):
            re, im = zr[i][j], zi[i][j]
            for k in range(j):
                re = re - (zr[i][k] * lr[j][k] + zi[i][k] * li[j][k])
                im = im - (zi[i][k] * lr[j][k] - zr[i][k] * li[j][k])
            zr[i][j], zi[i][j] = re, im
            lr[i][j], li[i][j] = re * recip[j], im * recip[j]
    mr = [[None] * n for _ in range(n)]
    mi = [[None] * n for _ in range(n)]
    for j in range(n):
        for i in range(j + 1, n):
            re, im = lr[i][j], li[i][j]
            for k in range(j + 1, i):
                re = re + (lr[i][k] * mr[k][j] - li[i][k] * mi[k][j])
                im = im + (lr[i][k] * mi[k][j] + li[i][k] * mr[k][j])
            mr[i][j], mi[i][j] = -re, -im
    p, q = {}, {}
    for i in range(n):
        for j in range(i, n):
            if i == j:
                re, im = recip[j], None
            else:
                re, im = mr[j][i] * recip[j], -(mi[j][i] * recip[j])
            for k in range(j + 1, n):
                sr, si = mr[k][j] * recip[k], mi[k][j] * recip[k]
                re = re + (mr[k][i] * sr + mi[k][i] * si)
                if i != j:
                    im = im + (mr[k][i] * si - mi[k][i] * sr)
            p[i, j] = re
            if i != j:
                q[i, j] = im
    return p, q


def gram_entries(t_ref):
    a, b = {}, {}
    for g in range(2):
        sa, sb = {}, {}
        for c in range(8):
            x = [t_ref[g * 4 + u, c * 8 : c * 8 + 8, :] for u in range(4)]
            y = [t_ref[g * 4 + u, 64 + c * 8 : 72 + c * 8, :] for u in range(4)]
            for u in range(4):
                for w in range(u, 4):
                    v = x[u] * x[w] + y[u] * y[w]
                    sa[u, w] = v if c == 0 else sa[u, w] + v
                    if w > u:
                        v = y[u] * x[w] - x[u] * y[w]
                        sb[u, w] = v if c == 0 else sb[u, w] + v
        for key in sa:
            a.setdefault(key, []).append(jnp.sum(sa[key], axis=0, keepdims=True))
        for key in sb:
            b.setdefault(key, []).append(jnp.sum(sb[key], axis=0, keepdims=True))
    a = {key: jnp.concatenate(a[key], axis=0) for key in a}
    b = {key: jnp.concatenate(b[key], axis=0) for key in b}
    return a, b


def inner_kernel(seq_ref, h_ref, labels_ref, noise_ref, x_ref, aux_ref):
    for f in range(128):
        m, at = divmod(f, 16)
        if 0 < f < 127:
            x_ref[m, at * 8 : at * 8 + 8, :] = 0.5 * h_ref[f] + 0.25 * (h_ref[f - 1] + h_ref[f + 1])
        else:
            near = h_ref[1] if f == 0 else h_ref[126]
            x_ref[m, at * 8 : at * 8 + 8, :] = 0.5 * h_ref[f] + 0.25 * near
    labels = labels_ref[...].astype(F32)
    labels = jnp.concatenate([labels, jnp.zeros((16, 128), F32)], axis=0).T
    for m in range(8):
        x_ref[m, 128:144, :] = labels[m * 16 : m * 16 + 16, :]
    noise = noise_ref[...]
    column = jnp.broadcast_to(noise, (128, 128)).T
    sub = lax.broadcasted_iota(jnp.int32, (128, 128), 0)
    lane = lax.broadcasted_iota(jnp.int32, (128, 128), 1)
    first = lax.axis_index("section") * 16
    spread = jnp.sum(jnp.where(sub == first + lane // 8, column, 0.0), axis=0, keepdims=True)
    position = 2 * (lane[:1] % 8) + (lane[:1] // 32) % 2
    wanted = jnp.zeros((1, 128), jnp.int32)
    for pos in range(16):
        wanted = jnp.where(position == pos, seq_ref[pos], wanted)
    aux_ref[...] = jnp.concatenate([noise, spread, wanted.astype(F32), jnp.zeros((5, 128), F32)], axis=0)


def edge_kernel(x_ref, close_ref, far_ref, out_ref):
    even = lax.axis_index("sc") % 2 == 0
    close, far = close_ref[0], far_ref[0]
    out_ref[...] = x_ref[...]
    out_ref[0, 0:8, :] = x_ref[0, 0:8, :] + 0.25 * jnp.where(even, far, close)
    out_ref[7, 120:128, :] = x_ref[7, 120:128, :] + 0.25 * jnp.where(even, close, far)


def add_kernel(x_ref, other_ref, order_ref, out_ref):
    out_ref[...] = x_ref[...] + other_ref[...]


def pack_kernel(x_ref, gain_ref, other_ref, out_ref, sum_ref):
    out_ref[...] = x_ref[...]
    sum_ref[...] = gain_ref[...] + other_ref[...]


def gain_kernel(x_ref, close_ref, far_ref, aux_ref, out_ref, t_ref):
    even = lax.axis_index("sc") % 2 == 0
    close, far = close_ref[0], far_ref[0]
    before = 0.25 * jnp.where(even, far, close)
    after = 0.25 * jnp.where(even, close, far)
    row = lax.broadcasted_iota(jnp.int32, (16, 128), 0)
    for i in range(8):
        rows = [x_ref[m, pl.ds(i, 16, stride=8), :] for m in range(8)]
        rows[0] = rows[0] + jnp.where(row == 0, before[i : i + 1], 0.0)
        rows[7] = rows[7] + jnp.where(row == 15, after[i : i + 1], 0.0)
        t_ref[i] = jnp.concatenate(rows, axis=0).T
    a, b = gram_entries(t_ref)
    noise = aux_ref[0:1]
    p, _ = hermitian_inverse(a, b, noise)
    out_ref[...] = jnp.concatenate([1.0 - noise * p[u, u] for u in range(4)], axis=0)


def filter_kernel(x_ref, aux_ref, order_ref, v_ref, w_ref, s_ref, t_ref, f_ref):
    for i in range(8):
        for f in range(16):
            v_ref[i, f * 8 : f * 8 + 8, :] = x_ref[pl.ds(f * 8 + i, 8, stride=144), :]
    for i in range(8):
        t_ref[i] = v_ref[i].T
    a, b = gram_entries(t_ref)
    p, q = hermitian_inverse(a, b, aux_ref[1:2])

    for g in range(2):
        pb = {key: jnp.broadcast_to(p[key][g : g + 1], (8, 128)) for key in p}
        qb = {key: jnp.broadcast_to(q[key][g : g + 1], (8, 128)) for key in q}
        for c in range(8):
            x = [t_ref[g * 4 + u, c * 8 : c * 8 + 8, :] for u in range(4)]
            y = [t_ref[g * 4 + u, 64 + c * 8 : 72 + c * 8, :] for u in range(4)]
            for u in range(4):
                fx = pb[u, u] * x[u]
                fy = pb[u, u] * y[u]
                for w in range(4):
                    if w != u:
                        key = (min(u, w), max(u, w))
                        fx = fx + pb[key] * x[w]
                        fy = fy + pb[key] * y[w]
                        if u < w:
                            fx = fx + qb[key] * y[w]
                            fy = fy - qb[key] * x[w]
                        else:
                            fx = fx - qb[key] * y[w]
                            fy = fy + qb[key] * x[w]
                f_ref[g * 4 + u, c * 8 : c * 8 + 8, :] = fx
                f_ref[g * 4 + u, 64 + c * 8 : 72 + c * 8, :] = fy
    for i in range(8):
        w_ref[i] = f_ref[i].T

    sub = lax.broadcasted_iota(jnp.int32, (128, 128), 0)
    lane = lax.broadcasted_iota(jnp.int32, (128, 128), 1)
    lane_u = (lane[:1] // 8) % 4
    wanted = aux_ref[2:3].astype(jnp.int32)
    row_u, row_g = sub % 4, (sub // 4) % 2
    own = lane[:16] // 8 == lax.broadcasted_iota(jnp.int32, (16, 128), 0)
    total = jnp.zeros((256, 128), F32)
    for m in range(8):
        pick = jnp.where((wanted == 2 * m + row_g) & (lane_u == row_u), 1.0, 0.0).astype(BF16)
        rows = []
        for f in range(16):
            at = m * 144 + 128 + f
            row = jnp.broadcast_to(x_ref[at : at + 1, :], (16, 128))
            rows.append(jnp.where(own, row, 0.0).astype(BF16))
        total = total + jnp.dot(jnp.concatenate(rows, axis=0), pick, preferred_element_type=F32)
    upper = jnp.floor(total * 0.25)
    re = 2.0 * (total - 4.0 * upper) - 3.0
    im = 2.0 * upper - 3.0
    for f in range(16):
        s_ref[f * 32 : f * 32 + 16, :] = re[f * 16 : f * 16 + 16]
        s_ref[f * 32 + 16 : f * 32 + 32, :] = im[f * 16 : f * 16 + 16]


def cancel_kernel(v_ref, w_ref, s_ref, y_ref, out_ref, ys_ref, yf_ref, e_ref, xz_ref, sem):
    first = pl.multiple_of(lax.axis_index("section") * 16, 16)
    copy = pltpu.make_async_copy(y_ref.at[:, pl.ds(first, 16), :], ys_ref.at[pl.ds(0, 14)], sem)
    copy.start()
    ys_ref[14:16] = jnp.zeros((2, 16, 128), F32)
    row = lax.broadcasted_iota(jnp.int32, (64, 128), 0)
    col = lax.broadcasted_iota(jnp.int32, (64, 128), 1)
    earlier = 2 * (row % 8) + row // 32 < 2 * (col % 8) + (col // 32) % 2
    sign = jnp.where(col[:1] < 64, -1.0, 1.0)
    copy.wait()
    yf_ref[...] = ys_ref[...].reshape(256, 128)
    nt = (((1,), (1,)), ((), ()))
    for f in range(16):
        at = slice(f * 8, f * 8 + 8)
        filt = jnp.concatenate([w_ref[i, at, :] for i in range(8)], axis=0)
        filt = jnp.concatenate([filt, pltpu.roll(filt, 64, 1) * sign], axis=0)
        fh = filt.astype(BF16)
        fl = (filt - fh.astype(F32)).astype(BF16)
        left = jnp.concatenate([v_ref[i, at, :] for i in range(8)] + [yf_ref[pl.ds(f, 16, stride=16), :]], axis=0)
        lh = left.astype(BF16)
        ll = (left - lh.astype(F32)).astype(BF16)
        xz = lax.dot_general(
            jnp.concatenate([lh, lh], axis=1), jnp.concatenate([fh, fl], axis=1), nt, preferred_element_type=F32
        )
        xz = xz + lax.dot_general(ll, fh, nt, preferred_element_type=F32)
        xz_ref[f, 0:64] = jnp.where(earlier, xz[:64], 0.0)
        xz_ref[f, 64:80] = xz[64:]
    for f in range(16):
        cross = xz_ref[f, 0:64]
        ch = cross.astype(BF16)
        cl = (cross - ch.astype(F32)).astype(BF16)
        sym = s_ref[f * 32 : f * 32 + 32, :].astype(BF16)
        gone = jnp.dot(sym, jnp.concatenate([ch, cl], axis=0), preferred_element_type=F32)
        gone = gone[:16] + pltpu.roll(gone[16:], 64, 1) * sign
        e_ref[pl.ds(f, 16, stride=16), :] = xz_ref[f, 64:80] - gone * (1.0 / ROOT_TEN)
    for half in range(2):
        turned = e_ref[half * 128 : half * 128 + 128, :].T
        for c in range(2):
            for g in range(2):
                for u in range(4):
                    at = (c * 8 + g * 4 + u) * 8
                    out_ref[pl.ds(half * 16 + g * 8 + c * 4 + u, 8, stride=32), :] = turned[at : at + 8, :]


def finish_kernel(count, est_ref, gain_ref, out_ref):
    total = jnp.sum(gain_ref[...], axis=1, keepdims=True)
    recip = count / total
    block = lax.broadcasted_iota(jnp.int32, (8, 128), 1) // 16
    for g in range(2):
        users = [recip[u * 2 + g : u * 2 + g + 1] for u in range(4)]
        scale = jnp.broadcast_to(jnp.concatenate(users + users, axis=0), (8, 128))
        for half in range(2):
            x = [est_ref[m, half, g * 8 : g * 8 + 8, :] for m in range(8)]
            for bit in (1, 2, 4):
                low = (block & bit) == 0
                new = list(x)
                for i in range(8):
                    if i & bit == 0:
                        j = i | bit
                        new[i] = jnp.where(low, x[i], pltpu.roll(x[j], 16 * bit, 1))
                        new[j] = jnp.where(low, pltpu.roll(x[i], 128 - 16 * bit, 1), x[j])
                x = new
            for i in range(8):
                t = half * 8 + i
                if t < 14:
                    out_ref[t, g * 8 : g * 8 + 8, :] = x[i] * scale


def halo(h):
    size = lax.axis_size("sc")
    even = lax.axis_index("sc") % 2 == 0
    close = [(i, i ^ 1) for i in range(size)]
    far = [(i, i + 1) for i in range(1, size - 1, 2)]
    far = far + [(j, i) for i, j in far]
    far = lax.ppermute(jnp.where(even, h[:1], h[-1:]), "sc", far)
    close = lax.ppermute(jnp.where(even, h[-1:], h[:1]), "sc", close)
    return close, far


def over_sections(x):
    return lax.all_to_all(x, "section", split_axis=0, concat_axis=0, tiled=True)


def from_partner(x, bit):
    return lax.ppermute(x, "sc", [(i, i ^ bit) for i in range(lax.axis_size("sc"))])


def kernel(body, shapes, in_specs, name, scratch=(), out_specs=None, aliases=None, flops=0, moved=0):
    out = pl.pallas_call(
        body,
        out_shape=[jax.ShapeDtypeStruct(shape, F32) for shape in shapes],
        in_specs=in_specs,
        out_specs=out_specs or [VMEM] * len(shapes),
        scratch_shapes=list(scratch),
        input_output_aliases=aliases or {},
        compiler_params=PARAMS,
        cost_estimate=pl.CostEstimate(flops=flops, bytes_accessed=moved, transcendentals=0),
        name=name,
    )
    return lambda *args: out(*args) if len(shapes) > 1 else out(*args)[0]


def local(observed_vector, propagation_matrix, noise_var, sliced_constellation, detection_sequence):
    h = propagation_matrix.reshape(128, 8, 128)
    noise = noise_var.reshape(1, 128)
    labels = sliced_constellation.transpose(1, 2, 0).reshape(112, 128)
    y = observed_vector.transpose(1, 0, 2)
    big = (8, 128, 128)
    close, far = halo(h)
    rows = (8, 144, 128)
    tile = (8, 128)
    near, aux = kernel(inner_kernel, [rows, tile], [SMEM] + [VMEM] * 3, "inner", flops=10**6, moved=2 * 10**6)(
        detection_sequence, h, labels, noise
    )
    gathered = over_sections(kernel(edge_kernel, [rows], [VMEM] * 3, "edge")(near, close, far))
    scratch = [pltpu.VMEM(big, F32)]
    gain = kernel(gain_kernel, [tile], [VMEM] * 4, "gain", scratch, flops=10**6, moved=10**6)(near, close, far, aux)
    gain = gain + from_partner(gain, 16)
    gain = kernel(add_kernel, [tile], [VMEM, VMEM, ANY], "add")(gain, from_partner(gain, 1), gathered)
    scratch = [pltpu.VMEM(big, F32), pltpu.VMEM(big, F32)]
    tiles, filters, symbols = kernel(
        filter_kernel, [big, big, (512, 128)], [VMEM, VMEM, ANY], "filters", scratch, flops=10**8, moved=4 * 10**6
    )(gathered.reshape(1152, 128), aux, gain)
    scratch = [pltpu.VMEM((16, 16, 128), F32), pltpu.VMEM((256, 128), F32), pltpu.VMEM((256, 128), F32)]
    scratch += [pltpu.VMEM((16, 80, 128), F32), pltpu.SemaphoreType.DMA]
    estimates = kernel(cancel_kernel, [(256, 128)], [VMEM, VMEM, VMEM, ANY], "cancel", scratch, flops=10**8, moved=4 * 10**6)(
        tiles, filters, symbols, y
    )
    estimates, gain = kernel(pack_kernel, [(256, 128), tile], [VMEM] * 3, "pack")(estimates, gain, from_partner(gain, 2))
    estimates = over_sections(estimates.reshape(8, 2, 16, 128))
    gain = kernel(add_kernel, [tile], [VMEM, VMEM, ANY], "add", flops=10**10, moved=10**8)(gain, from_partner(gain, 4), aux)
    gain = gain + from_partner(gain, 8)
    count = float(128 * lax.axis_size("sc"))
    body = lambda *refs: finish_kernel(count, *refs)
    out = kernel(body, [(14, 16, 128)], [VMEM] * 2, "finish")(estimates, gain)
    return out.transpose(2, 0, 1)


def solution(mesh):
    in_specs = (
        P("sc", None, None),
        P("sc", "section", None, None),
        P("sc"),
        P("sc", None, "section"),
        P(),
    )
    out_specs = P("sc", None, "section")
    return jax.shard_map(local, mesh=mesh, in_specs=in_specs, out_specs=out_specs, check_vma=False)
```

```python
import jax
import jax.numpy as jnp
from jax import lax
from jax.experimental import pallas as pl
from jax.experimental.pallas import tpu as pltpu
from jax.sharding import PartitionSpec as P

ROOT_TEN = 3.1622776601683795
F32 = jnp.float32
BF16 = jnp.bfloat16
VMEM = pl.BlockSpec(memory_space=pltpu.VMEM)
ANY = pl.BlockSpec(memory_space=pl.ANY)
SMEM = pl.BlockSpec(memory_space=pltpu.SMEM)
PARAMS = pltpu.CompilerParams(vmem_limit_bytes=32 * 1024 * 1024)


def hermitian_inverse(a, b, noise):
    n = 4
    zr = [[None] * n for _ in range(n)]
    zi = [[None] * n for _ in range(n)]
    for i in range(n):
        for j in range(i + 1):
            zr[i][j] = a[j, i] + noise if i == j else a[j, i]
            zi[i][j] = None if i == j else b[j, i]
    lr = [[None] * n for _ in range(n)]
    li = [[None] * n for _ in range(n)]
    recip = [None] * n
    for j in range(n):
        d = zr[j][j]
        for k in range(j):
            d = d - (zr[j][k] * lr[j][k] + zi[j][k] * li[j][k])
        recip[j] = 1.0 / d
        for i in range(j + 1, n):
            re, im = zr[i][j], zi[i][j]
            for k in range(j):
                re = re - (zr[i][k] * lr[j][k] + zi[i][k] * li[j][k])
                im = im - (zi[i][k] * lr[j][k] - zr[i][k] * li[j][k])
            zr[i][j], zi[i][j] = re, im
            lr[i][j], li[i][j] = re * recip[j], im * recip[j]
    mr = [[None] * n for _ in range(n)]
    mi = [[None] * n for _ in range(n)]
    for j in range(n):
        for i in range(j + 1, n):
            re, im = lr[i][j], li[i][j]
            for k in range(j + 1, i):
                re = re + (lr[i][k] * mr[k][j] - li[i][k] * mi[k][j])
                im = im + (lr[i][k] * mi[k][j] + li[i][k] * mr[k][j])
            mr[i][j], mi[i][j] = -re, -im
    p, q = {}, {}
    for i in range(n):
        for j in range(i, n):
            if i == j:
                re, im = recip[j], None
            else:
                re, im = mr[j][i] * recip[j], -(mi[j][i] * recip[j])
            for k in range(j + 1, n):
                sr, si = mr[k][j] * recip[k], mi[k][j] * recip[k]
                re = re + (mr[k][i] * sr + mi[k][i] * si)
                if i != j:
                    im = im + (mr[k][i] * si - mi[k][i] * sr)
            p[i, j] = re
            if i != j:
                q[i, j] = im
    return p, q


def gram_entries(t_ref):
    a, b = {}, {}
    for g in range(2):
        sa, sb = {}, {}
        for c in range(8):
            x = [t_ref[g * 4 + u, c * 8 : c * 8 + 8, :] for u in range(4)]
            y = [t_ref[g * 4 + u, 64 + c * 8 : 72 + c * 8, :] for u in range(4)]
            for u in range(4):
                for w in range(u, 4):
                    v = x[u] * x[w] + y[u] * y[w]
                    sa[u, w] = v if c == 0 else sa[u, w] + v
                    if w > u:
                        v = y[u] * x[w] - x[u] * y[w]
                        sb[u, w] = v if c == 0 else sb[u, w] + v
        for key in sa:
            a.setdefault(key, []).append(jnp.sum(sa[key], axis=0, keepdims=True))
        for key in sb:
            b.setdefault(key, []).append(jnp.sum(sb[key], axis=0, keepdims=True))
    a = {key: jnp.concatenate(a[key], axis=0) for key in a}
    b = {key: jnp.concatenate(b[key], axis=0) for key in b}
    return a, b


def inner_kernel(seq_ref, h_ref, labels_ref, noise_ref, x_ref, aux_ref):
    for f in range(128):
        m, at = divmod(f, 16)
        if 0 < f < 127:
            x_ref[m, at * 8 : at * 8 + 8, :] = 0.5 * h_ref[f] + 0.25 * (h_ref[f - 1] + h_ref[f + 1])
        else:
            near = h_ref[1] if f == 0 else h_ref[126]
            x_ref[m, at * 8 : at * 8 + 8, :] = 0.5 * h_ref[f] + 0.25 * near
    labels = labels_ref[...].astype(F32)
    labels = jnp.concatenate([labels, jnp.zeros((16, 128), F32)], axis=0).T
    for m in range(8):
        x_ref[m, 128:144, :] = labels[m * 16 : m * 16 + 16, :]
    noise = noise_ref[...]
    column = jnp.broadcast_to(noise, (128, 128)).T
    sub = lax.broadcasted_iota(jnp.int32, (128, 128), 0)
    lane = lax.broadcasted_iota(jnp.int32, (128, 128), 1)
    first = lax.axis_index("section") * 16
    spread = jnp.sum(jnp.where(sub == first + lane // 8, column, 0.0), axis=0, keepdims=True)
    position = 2 * (lane[:1] % 8) + (lane[:1] // 32) % 2
    wanted = jnp.zeros((1, 128), jnp.int32)
    for pos in range(16):
        wanted = jnp.where(position == pos, seq_ref[pos], wanted)
    aux_ref[...] = jnp.concatenate([noise, spread, wanted.astype(F32), jnp.zeros((5, 128), F32)], axis=0)


def edge_kernel(x_ref, close_ref, far_ref, out_ref):
    even = lax.axis_index("sc") % 2 == 0
    close, far = close_ref[0], far_ref[0]
    out_ref[...] = x_ref[...]
    out_ref[0, 0:8, :] = x_ref[0, 0:8, :] + 0.25 * jnp.where(even, far, close)
    out_ref[7, 120:128, :] = x_ref[7, 120:128, :] + 0.25 * jnp.where(even, close, far)


def add_kernel(x_ref, other_ref, order_ref, out_ref):
    out_ref[...] = x_ref[...] + other_ref[...]


def pack_kernel(x_ref, gain_ref, other_ref, out_ref, sum_ref):
    out_ref[...] = x_ref[...]
    sum_ref[...] = gain_ref[...] + other_ref[...]


def gain_kernel(x_ref, close_ref, far_ref, aux_ref, out_ref, t_ref):
    even = lax.axis_index("sc") % 2 == 0
    close, far = close_ref[0], far_ref[0]
    before = 0.25 * jnp.where(even, far, close)
    after = 0.25 * jnp.where(even, close, far)
    row = lax.broadcasted_iota(jnp.int32, (16, 128), 0)
    for i in range(8):
        rows = [x_ref[m, pl.ds(i, 16, stride=8), :] for m in range(8)]
        rows[0] = rows[0] + jnp.where(row == 0, before[i : i + 1], 0.0)
        rows[7] = rows[7] + jnp.where(row == 15, after[i : i + 1], 0.0)
        t_ref[i] = jnp.concatenate(rows, axis=0).T
    a, b = gram_entries(t_ref)
    noise = aux_ref[0:1]
    p, _ = hermitian_inverse(a, b, noise)
    out_ref[...] = jnp.concatenate([1.0 - noise * p[u, u] for u in range(4)], axis=0)


def filter_kernel(x_ref, aux_ref, order_ref, v_ref, w_ref, s_ref, t_ref, f_ref):
    for i in range(8):
        for f in range(16):
            v_ref[i, f * 8 : f * 8 + 8, :] = x_ref[pl.ds(f * 8 + i, 8, stride=144), :]
    for i in range(8):
        t_ref[i] = v_ref[i].T
    a, b = gram_entries(t_ref)
    p, q = hermitian_inverse(a, b, aux_ref[1:2])

    for g in range(2):
        pb = {key: jnp.broadcast_to(p[key][g : g + 1], (8, 128)) for key in p}
        qb = {key: jnp.broadcast_to(q[key][g : g + 1], (8, 128)) for key in q}
        for c in range(8):
            x = [t_ref[g * 4 + u, c * 8 : c * 8 + 8, :] for u in range(4)]
            y = [t_ref[g * 4 + u, 64 + c * 8 : 72 + c * 8, :] for u in range(4)]
            for u in range(4):
                fx = pb[u, u] * x[u]
                fy = pb[u, u] * y[u]
                for w in range(4):
                    if w != u:
                        key = (min(u, w), max(u, w))
                        fx = fx + pb[key] * x[w]
                        fy = fy + pb[key] * y[w]
                        if u < w:
                            fx = fx + qb[key] * y[w]
                            fy = fy - qb[key] * x[w]
                        else:
                            fx = fx - qb[key] * y[w]
                            fy = fy + qb[key] * x[w]
                f_ref[g * 4 + u, c * 8 : c * 8 + 8, :] = fx
                f_ref[g * 4 + u, 64 + c * 8 : 72 + c * 8, :] = fy
    for i in range(8):
        w_ref[i] = f_ref[i].T

    sub = lax.broadcasted_iota(jnp.int32, (128, 128), 0)
    lane = lax.broadcasted_iota(jnp.int32, (128, 128), 1)
    lane_u = (lane[:1] // 8) % 4
    wanted = aux_ref[2:3].astype(jnp.int32)
    row_u, row_g = sub % 4, (sub // 4) % 2
    own = lane[:16] // 8 == lax.broadcasted_iota(jnp.int32, (16, 128), 0)
    total = jnp.zeros((256, 128), F32)
    for m in range(8):
        pick = jnp.where((wanted == 2 * m + row_g) & (lane_u == row_u), 1.0, 0.0).astype(BF16)
        rows = []
        for f in range(16):
            at = m * 144 + 128 + f
            row = jnp.broadcast_to(x_ref[at : at + 1, :], (16, 128))
            rows.append(jnp.where(own, row, 0.0).astype(BF16))
        total = total + jnp.dot(jnp.concatenate(rows, axis=0), pick, preferred_element_type=F32)
    upper = jnp.floor(total * 0.25)
    re = 2.0 * (total - 4.0 * upper) - 3.0
    im = 2.0 * upper - 3.0
    for f in range(16):
        s_ref[f * 32 : f * 32 + 16, :] = re[f * 16 : f * 16 + 16]
        s_ref[f * 32 + 16 : f * 32 + 32, :] = im[f * 16 : f * 16 + 16]


def cancel_kernel(v_ref, w_ref, s_ref, y_ref, out_ref, ys_ref, yf_ref, e_ref, xz_ref, sem):
    first = pl.multiple_of(lax.axis_index("section") * 16, 16)
    copy = pltpu.make_async_copy(y_ref.at[:, pl.ds(first, 16), :], ys_ref.at[pl.ds(0, 14)], sem)
    copy.start()
    ys_ref[14:16] = jnp.zeros((2, 16, 128), F32)
    row = lax.broadcasted_iota(jnp.int32, (64, 128), 0)
    col = lax.broadcasted_iota(jnp.int32, (64, 128), 1)
    earlier = 2 * (row % 8) + row // 32 < 2 * (col % 8) + (col // 32) % 2
    sign = jnp.where(col[:1] < 64, -1.0, 1.0)
    copy.wait()
    yf_ref[...] = ys_ref[...].reshape(256, 128)
    nt = (((1,), (1,)), ((), ()))
    for f in range(16):
        at = slice(f * 8, f * 8 + 8)
        filt = jnp.concatenate([w_ref[i, at, :] for i in range(8)], axis=0)
        filt = jnp.concatenate([filt, pltpu.roll(filt, 64, 1) * sign], axis=0)
        fh = filt.astype(BF16)
        fl = (filt - fh.astype(F32)).astype(BF16)
        left = jnp.concatenate([v_ref[i, at, :] for i in range(8)] + [yf_ref[pl.ds(f, 16, stride=16), :]], axis=0)
        lh = left.astype(BF16)
        ll = (left - lh.astype(F32)).astype(BF16)
        xz = lax.dot_general(
            jnp.concatenate([lh, lh], axis=1), jnp.concatenate([fh, fl], axis=1), nt, preferred_element_type=F32
        )
        xz = xz + lax.dot_general(ll, fh, nt, preferred_element_type=F32)
        xz_ref[f, 0:64] = jnp.where(earlier, xz[:64], 0.0)
        xz_ref[f, 64:80] = xz[64:]
    for f in range(16):
        cross = xz_ref[f, 0:64]
        ch = cross.astype(BF16)
        cl = (cross - ch.astype(F32)).astype(BF16)
        sym = s_ref[f * 32 : f * 32 + 32, :].astype(BF16)
        gone = jnp.dot(sym, jnp.concatenate([ch, cl], axis=0), preferred_element_type=F32)
        gone = gone[:16] + pltpu.roll(gone[16:], 64, 1) * sign
        e_ref[pl.ds(f, 16, stride=16), :] = xz_ref[f, 64:80] - gone * (1.0 / ROOT_TEN)
    for half in range(2):
        turned = e_ref[half * 128 : half * 128 + 128, :].T
        for c in range(2):
            for g in range(2):
                for u in range(4):
                    at = (c * 8 + g * 4 + u) * 8
                    out_ref[pl.ds(half * 16 + g * 8 + c * 4 + u, 8, stride=32), :] = turned[at : at + 8, :]


def finish_kernel(count, est_ref, gain_ref, out_ref):
    total = jnp.sum(gain_ref[...], axis=1, keepdims=True)
    recip = count / total
    block = lax.broadcasted_iota(jnp.int32, (8, 128), 1) // 16
    for g in range(2):
        users = [recip[u * 2 + g : u * 2 + g + 1] for u in range(4)]
        scale = jnp.broadcast_to(jnp.concatenate(users + users, axis=0), (8, 128))
        for half in range(2):
            x = [est_ref[m, half, g * 8 : g * 8 + 8, :] for m in range(8)]
            for bit in (1, 2, 4):
                low = (block & bit) == 0
                new = list(x)
                for i in range(8):
                    if i & bit == 0:
                        j = i | bit
                        new[i] = jnp.where(low, x[i], pltpu.roll(x[j], 16 * bit, 1))
                        new[j] = jnp.where(low, pltpu.roll(x[i], 128 - 16 * bit, 1), x[j])
                x = new
            for i in range(8):
                t = half * 8 + i
                if t < 14:
                    out_ref[t, g * 8 : g * 8 + 8, :] = x[i] * scale


def halo(h):
    size = lax.axis_size("sc")
    even = lax.axis_index("sc") % 2 == 0
    close = [(i, i ^ 1) for i in range(size)]
    far = [(i, i + 1) for i in range(1, size - 1, 2)]
    far = far + [(j, i) for i, j in far]
    far = lax.ppermute(jnp.where(even, h[:1], h[-1:]), "sc", far)
    close = lax.ppermute(jnp.where(even, h[-1:], h[:1]), "sc", close)
    return close, far


def over_sections(x):
    return lax.all_to_all(x, "section", split_axis=0, concat_axis=0, tiled=True)


def from_partner(x, bit):
    code = [z ^ (z >> 1) for z in range(lax.axis_size("sc") // 4)]

    def partner(i):
        return i ^ bit if bit < 4 else code.index(code[i // 4] ^ (bit // 4)) * 4 + i % 4

    return lax.ppermute(x, "sc", [(i, partner(i)) for i in range(lax.axis_size("sc"))])


def kernel(body, shapes, in_specs, name, scratch=(), out_specs=None, aliases=None, flops=0, moved=0):
    out = pl.pallas_call(
        body,
        out_shape=[jax.ShapeDtypeStruct(shape, F32) for shape in shapes],
        in_specs=in_specs,
        out_specs=out_specs or [VMEM] * len(shapes),
        scratch_shapes=list(scratch),
        input_output_aliases=aliases or {},
        compiler_params=PARAMS,
        cost_estimate=pl.CostEstimate(flops=flops, bytes_accessed=moved, transcendentals=0),
        name=name,
    )
    return lambda *args: out(*args) if len(shapes) > 1 else out(*args)[0]


def local(observed_vector, propagation_matrix, noise_var, sliced_constellation, detection_sequence):
    h = propagation_matrix.reshape(128, 8, 128)
    noise = noise_var.reshape(1, 128)
    labels = sliced_constellation.transpose(1, 2, 0).reshape(112, 128)
    y = observed_vector.transpose(1, 0, 2)
    big = (8, 128, 128)
    close, far = halo(h)
    rows = (8, 144, 128)
    tile = (8, 128)
    near, aux = kernel(inner_kernel, [rows, tile], [SMEM] + [VMEM] * 3, "inner", flops=10**6, moved=2 * 10**6)(
        detection_sequence, h, labels, noise
    )
    gathered = over_sections(kernel(edge_kernel, [rows], [VMEM] * 3, "edge")(near, close, far))
    scratch = [pltpu.VMEM(big, F32)]
    gain = kernel(gain_kernel, [tile], [VMEM] * 4, "gain", scratch, flops=10**6, moved=10**6)(near, close, far, aux)
    gain = gain + from_partner(gain, 16)
    gain = kernel(add_kernel, [tile], [VMEM, VMEM, ANY], "add")(gain, from_partner(gain, 4), gathered)
    scratch = [pltpu.VMEM(big, F32), pltpu.VMEM(big, F32)]
    tiles, filters, symbols = kernel(
        filter_kernel, [big, big, (512, 128)], [VMEM, VMEM, ANY], "filters", scratch, flops=10**8, moved=4 * 10**6
    )(gathered.reshape(1152, 128), aux, gain)
    scratch = [pltpu.VMEM((16, 16, 128), F32), pltpu.VMEM((256, 128), F32), pltpu.VMEM((256, 128), F32)]
    scratch += [pltpu.VMEM((16, 80, 128), F32), pltpu.SemaphoreType.DMA]
    estimates = kernel(cancel_kernel, [(256, 128)], [VMEM, VMEM, VMEM, ANY], "cancel", scratch, flops=10**8, moved=4 * 10**6)(
        tiles, filters, symbols, y
    )
    estimates, gain = kernel(pack_kernel, [(256, 128), tile], [VMEM] * 3, "pack")(estimates, gain, from_partner(gain, 1))
    estimates = over_sections(estimates.reshape(8, 2, 16, 128))
    gain = kernel(add_kernel, [tile], [VMEM, VMEM, ANY], "add", flops=10**10, moved=10**8)(gain, from_partner(gain, 2), aux)
    gain = gain + from_partner(gain, 8)
    count = float(128 * lax.axis_size("sc"))
    body = lambda *refs: finish_kernel(count, *refs)
    out = kernel(body, [(14, 16, 128)], [VMEM] * 2, "finish")(estimates, gain)
    return out.transpose(2, 0, 1)


def solution(mesh):
    in_specs = (
        P("sc", None, None),
        P("sc", "section", None, None),
        P("sc"),
        P("sc", None, "section"),
        P(),
    )
    out_specs = P("sc", None, "section")
    return jax.shard_map(local, mesh=mesh, in_specs=in_specs, out_specs=out_specs, check_vma=False)
```

```python
import jax
import jax.numpy as jnp
from jax import lax
from jax.experimental import pallas as pl
from jax.experimental.pallas import tpu as pltpu
from jax.sharding import PartitionSpec as P

ROOT_TEN = 3.1622776601683795
F32 = jnp.float32
BF16 = jnp.bfloat16
VMEM = pl.BlockSpec(memory_space=pltpu.VMEM)
ANY = pl.BlockSpec(memory_space=pl.ANY)
SMEM = pl.BlockSpec(memory_space=pltpu.SMEM)
PARAMS = pltpu.CompilerParams(vmem_limit_bytes=32 * 1024 * 1024)


def hermitian_inverse(a, b, noise):
    n = 4
    zr = [[None] * n for _ in range(n)]
    zi = [[None] * n for _ in range(n)]
    for i in range(n):
        for j in range(i + 1):
            zr[i][j] = a[j, i] + noise if i == j else a[j, i]
            zi[i][j] = None if i == j else b[j, i]
    lr = [[None] * n for _ in range(n)]
    li = [[None] * n for _ in range(n)]
    recip = [None] * n
    for j in range(n):
        d = zr[j][j]
        for k in range(j):
            d = d - (zr[j][k] * lr[j][k] + zi[j][k] * li[j][k])
        recip[j] = 1.0 / d
        for i in range(j + 1, n):
            re, im = zr[i][j], zi[i][j]
            for k in range(j):
                re = re - (zr[i][k] * lr[j][k] + zi[i][k] * li[j][k])
                im = im - (zi[i][k] * lr[j][k] - zr[i][k] * li[j][k])
            zr[i][j], zi[i][j] = re, im
            lr[i][j], li[i][j] = re * recip[j], im * recip[j]
    mr = [[None] * n for _ in range(n)]
    mi = [[None] * n for _ in range(n)]
    for j in range(n):
        for i in range(j + 1, n):
            re, im = lr[i][j], li[i][j]
            for k in range(j + 1, i):
                re = re + (lr[i][k] * mr[k][j] - li[i][k] * mi[k][j])
                im = im + (lr[i][k] * mi[k][j] + li[i][k] * mr[k][j])
            mr[i][j], mi[i][j] = -re, -im
    p, q = {}, {}
    for i in range(n):
        for j in range(i, n):
            if i == j:
                re, im = recip[j], None
            else:
                re, im = mr[j][i] * recip[j], -(mi[j][i] * recip[j])
            for k in range(j + 1, n):
                sr, si = mr[k][j] * recip[k], mi[k][j] * recip[k]
                re = re + (mr[k][i] * sr + mi[k][i] * si)
                if i != j:
                    im = im + (mr[k][i] * si - mi[k][i] * sr)
            p[i, j] = re
            if i != j:
                q[i, j] = im
    return p, q


def gram_entries(t_ref):
    a, b = {}, {}
    for g in range(2):
        sa, sb = {}, {}
        for c in range(8):
            x = [t_ref[g * 4 + u, c * 8 : c * 8 + 8, :] for u in range(4)]
            y = [t_ref[g * 4 + u, 64 + c * 8 : 72 + c * 8, :] for u in range(4)]
            for u in range(4):
                for w in range(u, 4):
                    v = x[u] * x[w] + y[u] * y[w]
                    sa[u, w] = v if c == 0 else sa[u, w] + v
                    if w > u:
                        v = y[u] * x[w] - x[u] * y[w]
                        sb[u, w] = v if c == 0 else sb[u, w] + v
        for key in sa:
            a.setdefault(key, []).append(jnp.sum(sa[key], axis=0, keepdims=True))
        for key in sb:
            b.setdefault(key, []).append(jnp.sum(sb[key], axis=0, keepdims=True))
    a = {key: jnp.concatenate(a[key], axis=0) for key in a}
    b = {key: jnp.concatenate(b[key], axis=0) for key in b}
    return a, b


def inner_kernel(seq_ref, h_ref, labels_ref, noise_ref, x_ref, aux_ref):
    for f in range(128):
        m, at = divmod(f, 16)
        if 0 < f < 127:
            x_ref[m, at * 8 : at * 8 + 8, :] = 0.5 * h_ref[f] + 0.25 * (h_ref[f - 1] + h_ref[f + 1])
        else:
            near = h_ref[1] if f == 0 else h_ref[126]
            x_ref[m, at * 8 : at * 8 + 8, :] = 0.5 * h_ref[f] + 0.25 * near
    labels = labels_ref[...].astype(F32)
    labels = jnp.concatenate([labels, jnp.zeros((16, 128), F32)], axis=0).T
    for m in range(8):
        x_ref[m, 128:144, :] = labels[m * 16 : m * 16 + 16, :]
    noise = noise_ref[...]
    column = jnp.broadcast_to(noise, (128, 128)).T
    sub = lax.broadcasted_iota(jnp.int32, (128, 128), 0)
    lane = lax.broadcasted_iota(jnp.int32, (128, 128), 1)
    first = lax.axis_index("section") * 16
    spread = jnp.sum(jnp.where(sub == first + lane // 8, column, 0.0), axis=0, keepdims=True)
    position = 2 * (lane[:1] % 8) + (lane[:1] // 32) % 2
    wanted = jnp.zeros((1, 128), jnp.int32)
    for pos in range(16):
        wanted = jnp.where(position == pos, seq_ref[pos], wanted)
    aux_ref[...] = jnp.concatenate([noise, spread, wanted.astype(F32), jnp.zeros((5, 128), F32)], axis=0)


def edge_kernel(x_ref, close_ref, far_ref, out_ref, rows_ref, sem_ref):
    inside = pltpu.make_async_copy(x_ref.at[pl.ds(1, 6)], out_ref.at[pl.ds(1, 6)], sem_ref.at[0])
    inside.start()
    even = lax.axis_index("sc") % 2 == 0
    close, far = close_ref[0], far_ref[0]
    rows_ref[0] = x_ref[0]
    rows_ref[0, 0:8, :] = x_ref[0, 0:8, :] + 0.25 * jnp.where(even, far, close)
    first = pltpu.make_async_copy(rows_ref.at[0], out_ref.at[0], sem_ref.at[1])
    first.start()
    rows_ref[1] = x_ref[7]
    rows_ref[1, 120:128, :] = x_ref[7, 120:128, :] + 0.25 * jnp.where(even, close, far)
    last = pltpu.make_async_copy(rows_ref.at[1], out_ref.at[7], sem_ref.at[2])
    last.start()
    inside.wait()
    first.wait()
    last.wait()


def add_kernel(x_ref, other_ref, order_ref, out_ref):
    out_ref[...] = x_ref[...] + other_ref[...]


def pack_kernel(x_ref, gain_ref, other_ref, out_ref, sum_ref):
    out_ref[...] = x_ref[...]
    sum_ref[...] = gain_ref[...] + other_ref[...]


def gain_kernel(x_ref, close_ref, far_ref, aux_ref, out_ref, t_ref):
    even = lax.axis_index("sc") % 2 == 0
    close, far = close_ref[0], far_ref[0]
    before = 0.25 * jnp.where(even, far, close)
    after = 0.25 * jnp.where(even, close, far)
    row = lax.broadcasted_iota(jnp.int32, (16, 128), 0)
    for i in range(8):
        rows = [x_ref[m, pl.ds(i, 16, stride=8), :] for m in range(8)]
        rows[0] = rows[0] + jnp.where(row == 0, before[i : i + 1], 0.0)
        rows[7] = rows[7] + jnp.where(row == 15, after[i : i + 1], 0.0)
        t_ref[i] = jnp.concatenate(rows, axis=0).T
    a, b = gram_entries(t_ref)
    noise = aux_ref[0:1]
    p, _ = hermitian_inverse(a, b, noise)
    out_ref[...] = jnp.concatenate([1.0 - noise * p[u, u] for u in range(4)], axis=0)


def filter_kernel(x_ref, aux_ref, order_ref, v_ref, w_ref, s_ref, t_ref, f_ref):
    for i in range(8):
        for f in range(16):
            v_ref[i, f * 8 : f * 8 + 8, :] = x_ref[pl.ds(f * 8 + i, 8, stride=144), :]
    for i in range(8):
        t_ref[i] = v_ref[i].T
    a, b = gram_entries(t_ref)
    p, q = hermitian_inverse(a, b, aux_ref[1:2])

    for g in range(2):
        pb = {key: jnp.broadcast_to(p[key][g : g + 1], (8, 128)) for key in p}
        qb = {key: jnp.broadcast_to(q[key][g : g + 1], (8, 128)) for key in q}
        for c in range(8):
            x = [t_ref[g * 4 + u, c * 8 : c * 8 + 8, :] for u in range(4)]
            y = [t_ref[g * 4 + u, 64 + c * 8 : 72 + c * 8, :] for u in range(4)]
            for u in range(4):
                fx = pb[u, u] * x[u]
                fy = pb[u, u] * y[u]
                for w in range(4):
                    if w != u:
                        key = (min(u, w), max(u, w))
                        fx = fx + pb[key] * x[w]
                        fy = fy + pb[key] * y[w]
                        if u < w:
                            fx = fx + qb[key] * y[w]
                            fy = fy - qb[key] * x[w]
                        else:
                            fx = fx - qb[key] * y[w]
                            fy = fy + qb[key] * x[w]
                f_ref[g * 4 + u, c * 8 : c * 8 + 8, :] = fx
                f_ref[g * 4 + u, 64 + c * 8 : 72 + c * 8, :] = fy
    for i in range(8):
        w_ref[i] = f_ref[i].T

    sub = lax.broadcasted_iota(jnp.int32, (128, 128), 0)
    lane = lax.broadcasted_iota(jnp.int32, (128, 128), 1)
    lane_u = (lane[:1] // 8) % 4
    wanted = aux_ref[2:3].astype(jnp.int32)
    row_u, row_g = sub % 4, (sub // 4) % 2
    own = lane[:16] // 8 == lax.broadcasted_iota(jnp.int32, (16, 128), 0)
    total = jnp.zeros((256, 128), F32)
    for m in range(8):
        pick = jnp.where((wanted == 2 * m + row_g) & (lane_u == row_u), 1.0, 0.0).astype(BF16)
        rows = []
        for f in range(16):
            at = m * 144 + 128 + f
            row = jnp.broadcast_to(x_ref[at : at + 1, :], (16, 128))
            rows.append(jnp.where(own, row, 0.0).astype(BF16))
        total = total + jnp.dot(jnp.concatenate(rows, axis=0), pick, preferred_element_type=F32)
    upper = jnp.floor(total * 0.25)
    re = 2.0 * (total - 4.0 * upper) - 3.0
    im = 2.0 * upper - 3.0
    for f in range(16):
        s_ref[f * 32 : f * 32 + 16, :] = re[f * 16 : f * 16 + 16]
        s_ref[f * 32 + 16 : f * 32 + 32, :] = im[f * 16 : f * 16 + 16]


def cancel_kernel(v_ref, w_ref, s_ref, y_ref, out_ref, ys_ref, yf_ref, e_ref, xz_ref, sem):
    first = pl.multiple_of(lax.axis_index("section") * 16, 16)
    copy = pltpu.make_async_copy(y_ref.at[:, pl.ds(first, 16), :], ys_ref.at[pl.ds(0, 14)], sem)
    copy.start()
    ys_ref[14:16] = jnp.zeros((2, 16, 128), F32)
    row = lax.broadcasted_iota(jnp.int32, (64, 128), 0)
    col = lax.broadcasted_iota(jnp.int32, (64, 128), 1)
    earlier = 2 * (row % 8) + row // 32 < 2 * (col % 8) + (col // 32) % 2
    sign = jnp.where(col[:1] < 64, -1.0, 1.0)
    copy.wait()
    yf_ref[...] = ys_ref[...].reshape(256, 128)
    nt = (((1,), (1,)), ((), ()))
    for f in range(16):
        at = slice(f * 8, f * 8 + 8)
        filt = jnp.concatenate([w_ref[i, at, :] for i in range(8)], axis=0)
        filt = jnp.concatenate([filt, pltpu.roll(filt, 64, 1) * sign], axis=0)
        fh = filt.astype(BF16)
        fl = (filt - fh.astype(F32)).astype(BF16)
        left = jnp.concatenate([v_ref[i, at, :] for i in range(8)] + [yf_ref[pl.ds(f, 16, stride=16), :]], axis=0)
        lh = left.astype(BF16)
        ll = (left - lh.astype(F32)).astype(BF16)
        xz = lax.dot_general(
            jnp.concatenate([lh, lh], axis=1), jnp.concatenate([fh, fl], axis=1), nt, preferred_element_type=F32
        )
        xz = xz + lax.dot_general(ll, fh, nt, preferred_element_type=F32)
        xz_ref[f, 0:64] = jnp.where(earlier, xz[:64], 0.0)
        xz_ref[f, 64:80] = xz[64:]
    for f in range(16):
        cross = xz_ref[f, 0:64]
        ch = cross.astype(BF16)
        cl = (cross - ch.astype(F32)).astype(BF16)
        sym = s_ref[f * 32 : f * 32 + 32, :].astype(BF16)
        gone = jnp.dot(sym, jnp.concatenate([ch, cl], axis=0), preferred_element_type=F32)
        gone = gone[:16] + pltpu.roll(gone[16:], 64, 1) * sign
        e_ref[pl.ds(f, 16, stride=16), :] = xz_ref[f, 64:80] - gone * (1.0 / ROOT_TEN)
    for half in range(2):
        turned = e_ref[half * 128 : half * 128 + 128, :].T
        for c in range(2):
            for g in range(2):
                for u in range(4):
                    at = (c * 8 + g * 4 + u) * 8
                    out_ref[pl.ds(half * 16 + g * 8 + c * 4 + u, 8, stride=32), :] = turned[at : at + 8, :]


def finish_kernel(count, est_ref, gain_ref, out_ref, rows_ref, sem_ref):
    total = jnp.sum(gain_ref[...], axis=1, keepdims=True)
    recip = count / total
    block = lax.broadcasted_iota(jnp.int32, (8, 128), 1) // 16
    copies = []
    for half in range(2):
        for g in range(2):
            users = [recip[u * 2 + g : u * 2 + g + 1] for u in range(4)]
            scale = jnp.broadcast_to(jnp.concatenate(users + users, axis=0), (8, 128))
            x = [est_ref[m, half, g * 8 : g * 8 + 8, :] for m in range(8)]
            for bit in (1, 2, 4):
                low = (block & bit) == 0
                new = list(x)
                for i in range(8):
                    if i & bit == 0:
                        j = i | bit
                        new[i] = jnp.where(low, x[i], pltpu.roll(x[j], 16 * bit, 1))
                        new[j] = jnp.where(low, pltpu.roll(x[i], 128 - 16 * bit, 1), x[j])
                x = new
            for i in range(8 - 2 * half):
                rows_ref[half * 8 + i, g * 8 : g * 8 + 8, :] = x[i] * scale
        times = pl.ds(half * 8, 8 - 2 * half)
        copies.append(pltpu.make_async_copy(rows_ref.at[times], out_ref.at[times], sem_ref.at[half]))
        copies[half].start()
    for copy in copies:
        copy.wait()


def halo(h):
    size = lax.axis_size("sc")
    even = lax.axis_index("sc") % 2 == 0
    close = [(i, i ^ 1) for i in range(size)]
    far = [(i, i + 1) for i in range(1, size - 1, 2)]
    far = far + [(j, i) for i, j in far]
    far = lax.ppermute(jnp.where(even, h[:1], h[-1:]), "sc", far)
    close = lax.ppermute(jnp.where(even, h[-1:], h[:1]), "sc", close)
    return close, far


def over_sections(x):
    return lax.all_to_all(x, "section", split_axis=0, concat_axis=0, tiled=True)


def from_partner(x, bit):
    code = [z ^ (z >> 1) for z in range(lax.axis_size("sc") // 4)]

    def partner(i):
        return i ^ bit if bit < 4 else code.index(code[i // 4] ^ (bit // 4)) * 4 + i % 4

    return lax.ppermute(x, "sc", [(i, partner(i)) for i in range(lax.axis_size("sc"))])


def kernel(body, shapes, in_specs, name, scratch=(), out_specs=None, aliases=None, flops=0, moved=0):
    out = pl.pallas_call(
        body,
        out_shape=[jax.ShapeDtypeStruct(shape, F32) for shape in shapes],
        in_specs=in_specs,
        out_specs=out_specs or [VMEM] * len(shapes),
        scratch_shapes=list(scratch),
        input_output_aliases=aliases or {},
        compiler_params=PARAMS,
        cost_estimate=pl.CostEstimate(flops=flops, bytes_accessed=moved, transcendentals=0),
        name=name,
    )
    return lambda *args: out(*args) if len(shapes) > 1 else out(*args)[0]


def local(observed_vector, propagation_matrix, noise_var, sliced_constellation, detection_sequence):
    h = propagation_matrix.reshape(128, 8, 128)
    noise = noise_var.reshape(1, 128)
    labels = sliced_constellation.transpose(1, 2, 0).reshape(112, 128)
    y = observed_vector.transpose(1, 0, 2)
    big = (8, 128, 128)
    close, far = halo(h)
    rows = (8, 144, 128)
    tile = (8, 128)
    near, aux = kernel(inner_kernel, [rows, tile], [SMEM] + [VMEM] * 3, "inner", flops=10**6, moved=2 * 10**6)(
        detection_sequence, h, labels, noise
    )
    scratch = [pltpu.VMEM((2, 144, 128), F32), pltpu.SemaphoreType.DMA((3,))]
    gathered = over_sections(kernel(edge_kernel, [rows], [VMEM] * 3, "edge", scratch, [ANY])(near, close, far))
    scratch = [pltpu.VMEM(big, F32)]
    gain = kernel(gain_kernel, [tile], [VMEM] * 4, "gain", scratch, flops=10**6, moved=10**6)(near, close, far, aux)
    gain = gain + from_partner(gain, 16)
    gain = kernel(add_kernel, [tile], [VMEM, VMEM, ANY], "add")(gain, from_partner(gain, 4), gathered)
    scratch = [pltpu.VMEM(big, F32), pltpu.VMEM(big, F32)]
    tiles, filters, symbols = kernel(
        filter_kernel, [big, big, (512, 128)], [VMEM, VMEM, ANY], "filters", scratch, flops=10**8, moved=4 * 10**6
    )(gathered.reshape(1152, 128), aux, gain)
    scratch = [pltpu.VMEM((16, 16, 128), F32), pltpu.VMEM((256, 128), F32), pltpu.VMEM((256, 128), F32)]
    scratch += [pltpu.VMEM((16, 80, 128), F32), pltpu.SemaphoreType.DMA]
    estimates = kernel(cancel_kernel, [(256, 128)], [VMEM, VMEM, VMEM, ANY], "cancel", scratch, flops=10**8, moved=4 * 10**6)(
        tiles, filters, symbols, y
    )
    estimates, gain = kernel(pack_kernel, [(256, 128), tile], [VMEM] * 3, "pack")(estimates, gain, from_partner(gain, 1))
    estimates = over_sections(estimates.reshape(8, 2, 16, 128))
    gain = kernel(add_kernel, [tile], [VMEM, VMEM, ANY], "add", flops=10**10, moved=10**8)(gain, from_partner(gain, 2), aux)
    gain = gain + from_partner(gain, 8)
    count = float(128 * lax.axis_size("sc"))
    body = lambda *refs: finish_kernel(count, *refs)
    out = kernel(body, [(14, 16, 128)], [VMEM] * 2, "finish", [pltpu.VMEM((14, 16, 128), F32), pltpu.SemaphoreType.DMA((2,))], [ANY])(estimates, gain)
    return out.transpose(2, 0, 1)


def solution(mesh):
    in_specs = (
        P("sc", None, None),
        P("sc", "section", None, None),
        P("sc"),
        P("sc", None, "section"),
        P(),
    )
    out_specs = P("sc", None, "section")
    return jax.shard_map(local, mesh=mesh, in_specs=in_specs, out_specs=out_specs, check_vma=False)
```

```python
import jax
import jax.numpy as jnp
from jax import lax
from jax.experimental import pallas as pl
from jax.experimental.pallas import tpu as pltpu
from jax.sharding import PartitionSpec as P

ROOT_TEN = 3.1622776601683795
F32 = jnp.float32
BF16 = jnp.bfloat16
VMEM = pl.BlockSpec(memory_space=pltpu.VMEM)
ANY = pl.BlockSpec(memory_space=pl.ANY)
SMEM = pl.BlockSpec(memory_space=pltpu.SMEM)
PARAMS = pltpu.CompilerParams(vmem_limit_bytes=32 * 1024 * 1024)


def hermitian_inverse(a, b, noise):
    n = 4
    zr = [[None] * n for _ in range(n)]
    zi = [[None] * n for _ in range(n)]
    for i in range(n):
        for j in range(i + 1):
            zr[i][j] = a[j, i] + noise if i == j else a[j, i]
            zi[i][j] = None if i == j else b[j, i]
    lr = [[None] * n for _ in range(n)]
    li = [[None] * n for _ in range(n)]
    recip = [None] * n
    for j in range(n):
        d = zr[j][j]
        for k in range(j):
            d = d - (zr[j][k] * lr[j][k] + zi[j][k] * li[j][k])
        recip[j] = 1.0 / d
        for i in range(j + 1, n):
            re, im = zr[i][j], zi[i][j]
            for k in range(j):
                re = re - (zr[i][k] * lr[j][k] + zi[i][k] * li[j][k])
                im = im - (zi[i][k] * lr[j][k] - zr[i][k] * li[j][k])
            zr[i][j], zi[i][j] = re, im
            lr[i][j], li[i][j] = re * recip[j], im * recip[j]
    mr = [[None] * n for _ in range(n)]
    mi = [[None] * n for _ in range(n)]
    for j in range(n):
        for i in range(j + 1, n):
            re, im = lr[i][j], li[i][j]
            for k in range(j + 1, i):
                re = re + (lr[i][k] * mr[k][j] - li[i][k] * mi[k][j])
                im = im + (lr[i][k] * mi[k][j] + li[i][k] * mr[k][j])
            mr[i][j], mi[i][j] = -re, -im
    p, q = {}, {}
    for i in range(n):
        for j in range(i, n):
            if i == j:
                re, im = recip[j], None
            else:
                re, im = mr[j][i] * recip[j], -(mi[j][i] * recip[j])
            for k in range(j + 1, n):
                sr, si = mr[k][j] * recip[k], mi[k][j] * recip[k]
                re = re + (mr[k][i] * sr + mi[k][i] * si)
                if i != j:
                    im = im + (mr[k][i] * si - mi[k][i] * sr)
            p[i, j] = re
            if i != j:
                q[i, j] = im
    return p, q


def gram_entries(t_ref):
    a, b = {}, {}
    for g in range(2):
        sa, sb = {}, {}
        for c in range(8):
            x = [t_ref[g * 4 + u, c * 8 : c * 8 + 8, :] for u in range(4)]
            y = [t_ref[g * 4 + u, 64 + c * 8 : 72 + c * 8, :] for u in range(4)]
            for u in range(4):
                for w in range(u, 4):
                    v = x[u] * x[w] + y[u] * y[w]
                    sa[u, w] = v if c == 0 else sa[u, w] + v
                    if w > u:
                        v = y[u] * x[w] - x[u] * y[w]
                        sb[u, w] = v if c == 0 else sb[u, w] + v
        for key in sa:
            a.setdefault(key, []).append(jnp.sum(sa[key], axis=0, keepdims=True))
        for key in sb:
            b.setdefault(key, []).append(jnp.sum(sb[key], axis=0, keepdims=True))
    a = {key: jnp.concatenate(a[key], axis=0) for key in a}
    b = {key: jnp.concatenate(b[key], axis=0) for key in b}
    return a, b


def inner_kernel(seq_ref, h_ref, labels_ref, noise_ref, x_ref, aux_ref):
    for f in range(128):
        m, at = divmod(f, 16)
        if 0 < f < 127:
            x_ref[m, at * 8 : at * 8 + 8, :] = 0.5 * h_ref[f] + 0.25 * (h_ref[f - 1] + h_ref[f + 1])
        else:
            near = h_ref[1] if f == 0 else h_ref[126]
            x_ref[m, at * 8 : at * 8 + 8, :] = 0.5 * h_ref[f] + 0.25 * near
    labels = labels_ref[...].astype(F32)
    labels = jnp.concatenate([labels, jnp.zeros((16, 128), F32)], axis=0).T
    for m in range(8):
        x_ref[m, 128:144, :] = labels[m * 16 : m * 16 + 16, :]
    noise = noise_ref[...]
    column = jnp.broadcast_to(noise, (128, 128)).T
    sub = lax.broadcasted_iota(jnp.int32, (128, 128), 0)
    lane = lax.broadcasted_iota(jnp.int32, (128, 128), 1)
    first = lax.axis_index("section") * 16
    spread = jnp.sum(jnp.where(sub == first + lane // 8, column, 0.0), axis=0, keepdims=True)
    position = 2 * (lane[:1] % 8) + (lane[:1] // 32) % 2
    wanted = jnp.zeros((1, 128), jnp.int32)
    for pos in range(16):
        wanted = jnp.where(position == pos, seq_ref[pos], wanted)
    aux_ref[...] = jnp.concatenate([noise, spread, wanted.astype(F32), jnp.zeros((5, 128), F32)], axis=0)


def edge_kernel(x_ref, close_ref, far_ref, out_ref, rows_ref, sem_ref):
    inside = pltpu.make_async_copy(x_ref.at[pl.ds(1, 6)], out_ref.at[pl.ds(1, 6)], sem_ref.at[0])
    inside.start()
    even = lax.axis_index("sc") % 2 == 0
    close, far = close_ref[0], far_ref[0]
    rows_ref[0] = x_ref[0]
    rows_ref[0, 0:8, :] = x_ref[0, 0:8, :] + 0.25 * jnp.where(even, far, close)
    first = pltpu.make_async_copy(rows_ref.at[0], out_ref.at[0], sem_ref.at[1])
    first.start()
    rows_ref[1] = x_ref[7]
    rows_ref[1, 120:128, :] = x_ref[7, 120:128, :] + 0.25 * jnp.where(even, close, far)
    last = pltpu.make_async_copy(rows_ref.at[1], out_ref.at[7], sem_ref.at[2])
    last.start()
    inside.wait()
    first.wait()
    last.wait()


def add_kernel(x_ref, other_ref, order_ref, out_ref):
    out_ref[...] = x_ref[...] + other_ref[...]


def pack_kernel(x_ref, gain_ref, other_ref, out_ref, sum_ref):
    out_ref[...] = x_ref[...]
    sum_ref[...] = gain_ref[...] + other_ref[...]


def gain_kernel(x_ref, close_ref, far_ref, aux_ref, out_ref, t_ref):
    even = lax.axis_index("sc") % 2 == 0
    close, far = close_ref[0], far_ref[0]
    before = 0.25 * jnp.where(even, far, close)
    after = 0.25 * jnp.where(even, close, far)
    row = lax.broadcasted_iota(jnp.int32, (16, 128), 0)
    for i in range(8):
        rows = [x_ref[m, pl.ds(i, 16, stride=8), :] for m in range(8)]
        rows[0] = rows[0] + jnp.where(row == 0, before[i : i + 1], 0.0)
        rows[7] = rows[7] + jnp.where(row == 15, after[i : i + 1], 0.0)
        t_ref[i] = jnp.concatenate(rows, axis=0).T
    a, b = gram_entries(t_ref)
    noise = aux_ref[0:1]
    p, _ = hermitian_inverse(a, b, noise)
    out_ref[...] = jnp.concatenate([1.0 - noise * p[u, u] for u in range(4)], axis=0)


def filter_kernel(x_ref, aux_ref, v_ref, w_ref, s_ref, t_ref, f_ref):
    for i in range(8):
        for f in range(16):
            v_ref[i, f * 8 : f * 8 + 8, :] = x_ref[pl.ds(f * 8 + i, 8, stride=144), :]
    for i in range(8):
        t_ref[i] = v_ref[i].T
    a, b = gram_entries(t_ref)
    p, q = hermitian_inverse(a, b, aux_ref[1:2])

    for g in range(2):
        pb = {key: jnp.broadcast_to(p[key][g : g + 1], (8, 128)) for key in p}
        qb = {key: jnp.broadcast_to(q[key][g : g + 1], (8, 128)) for key in q}
        for c in range(8):
            x = [t_ref[g * 4 + u, c * 8 : c * 8 + 8, :] for u in range(4)]
            y = [t_ref[g * 4 + u, 64 + c * 8 : 72 + c * 8, :] for u in range(4)]
            for u in range(4):
                fx = pb[u, u] * x[u]
                fy = pb[u, u] * y[u]
                for w in range(4):
                    if w != u:
                        key = (min(u, w), max(u, w))
                        fx = fx + pb[key] * x[w]
                        fy = fy + pb[key] * y[w]
                        if u < w:
                            fx = fx + qb[key] * y[w]
                            fy = fy - qb[key] * x[w]
                        else:
                            fx = fx - qb[key] * y[w]
                            fy = fy + qb[key] * x[w]
                f_ref[g * 4 + u, c * 8 : c * 8 + 8, :] = fx
                f_ref[g * 4 + u, 64 + c * 8 : 72 + c * 8, :] = fy
    for i in range(8):
        w_ref[i] = f_ref[i].T

    sub = lax.broadcasted_iota(jnp.int32, (128, 128), 0)
    lane = lax.broadcasted_iota(jnp.int32, (128, 128), 1)
    lane_u = (lane[:1] // 8) % 4
    wanted = aux_ref[2:3].astype(jnp.int32)
    row_u, row_g = sub % 4, (sub // 4) % 2
    own = lane[:16] // 8 == lax.broadcasted_iota(jnp.int32, (16, 128), 0)
    total = jnp.zeros((256, 128), F32)
    for m in range(8):
        pick = jnp.where((wanted == 2 * m + row_g) & (lane_u == row_u), 1.0, 0.0).astype(BF16)
        rows = []
        for f in range(16):
            at = m * 144 + 128 + f
            row = jnp.broadcast_to(x_ref[at : at + 1, :], (16, 128))
            rows.append(jnp.where(own, row, 0.0).astype(BF16))
        total = total + jnp.dot(jnp.concatenate(rows, axis=0), pick, preferred_element_type=F32)
    upper = jnp.floor(total * 0.25)
    re = 2.0 * (total - 4.0 * upper) - 3.0
    im = 2.0 * upper - 3.0
    for f in range(16):
        s_ref[f * 32 : f * 32 + 16, :] = re[f * 16 : f * 16 + 16]
        s_ref[f * 32 + 16 : f * 32 + 32, :] = im[f * 16 : f * 16 + 16]


def cancel_kernel(v_ref, w_ref, s_ref, y_ref, out_ref, ys_ref, yf_ref, e_ref, xz_ref, sem):
    first = pl.multiple_of(lax.axis_index("section") * 16, 16)
    copy = pltpu.make_async_copy(y_ref.at[:, pl.ds(first, 16), :], ys_ref.at[pl.ds(0, 14)], sem)
    copy.start()
    ys_ref[14:16] = jnp.zeros((2, 16, 128), F32)
    row = lax.broadcasted_iota(jnp.int32, (64, 128), 0)
    col = lax.broadcasted_iota(jnp.int32, (64, 128), 1)
    earlier = 2 * (row % 8) + row // 32 < 2 * (col % 8) + (col // 32) % 2
    sign = jnp.where(col[:1] < 64, -1.0, 1.0)
    copy.wait()
    yf_ref[...] = ys_ref[...].reshape(256, 128)
    nt = (((1,), (1,)), ((), ()))
    for f in range(16):
        at = slice(f * 8, f * 8 + 8)
        filt = jnp.concatenate([w_ref[i, at, :] for i in range(8)], axis=0)
        filt = jnp.concatenate([filt, pltpu.roll(filt, 64, 1) * sign], axis=0)
        fh = filt.astype(BF16)
        fl = (filt - fh.astype(F32)).astype(BF16)
        left = jnp.concatenate([v_ref[i, at, :] for i in range(8)] + [yf_ref[pl.ds(f, 16, stride=16), :]], axis=0)
        lh = left.astype(BF16)
        ll = (left - lh.astype(F32)).astype(BF16)
        xz = lax.dot_general(
            jnp.concatenate([lh, lh], axis=1), jnp.concatenate([fh, fl], axis=1), nt, preferred_element_type=F32
        )
        xz = xz + lax.dot_general(ll, fh, nt, preferred_element_type=F32)
        xz_ref[f, 0:64] = jnp.where(earlier, xz[:64], 0.0)
        xz_ref[f, 64:80] = xz[64:]
    for f in range(16):
        cross = xz_ref[f, 0:64]
        ch = cross.astype(BF16)
        cl = (cross - ch.astype(F32)).astype(BF16)
        sym = s_ref[f * 32 : f * 32 + 32, :].astype(BF16)
        gone = jnp.dot(sym, jnp.concatenate([ch, cl], axis=0), preferred_element_type=F32)
        gone = gone[:16] + pltpu.roll(gone[16:], 64, 1) * sign
        e_ref[pl.ds(f, 16, stride=16), :] = xz_ref[f, 64:80] - gone * (1.0 / ROOT_TEN)
    for half in range(2):
        turned = e_ref[half * 128 : half * 128 + 128, :].T
        for c in range(2):
            for g in range(2):
                for u in range(4):
                    at = (c * 8 + g * 4 + u) * 8
                    out_ref[pl.ds(half * 16 + g * 8 + c * 4 + u, 8, stride=32), :] = turned[at : at + 8, :]


def finish_kernel(count, est_ref, gain_ref, out_ref, rows_ref, sem_ref):
    total = jnp.sum(gain_ref[...], axis=1, keepdims=True)
    recip = count / total
    block = lax.broadcasted_iota(jnp.int32, (8, 128), 1) // 16
    copies = []
    for half in range(2):
        for g in range(2):
            users = [recip[u * 2 + g : u * 2 + g + 1] for u in range(4)]
            scale = jnp.broadcast_to(jnp.concatenate(users + users, axis=0), (8, 128))
            x = [est_ref[m, half, g * 8 : g * 8 + 8, :] for m in range(8)]
            for bit in (1, 2, 4):
                low = (block & bit) == 0
                new = list(x)
                for i in range(8):
                    if i & bit == 0:
                        j = i | bit
                        new[i] = jnp.where(low, x[i], pltpu.roll(x[j], 16 * bit, 1))
                        new[j] = jnp.where(low, pltpu.roll(x[i], 128 - 16 * bit, 1), x[j])
                x = new
            for i in range(8 - 2 * half):
                rows_ref[half * 8 + i, g * 8 : g * 8 + 8, :] = x[i] * scale
        times = pl.ds(half * 8, 8 - 2 * half)
        copies.append(pltpu.make_async_copy(rows_ref.at[times], out_ref.at[times], sem_ref.at[half]))
        copies[half].start()
    for copy in copies:
        copy.wait()


def halo(h):
    size = lax.axis_size("sc")
    even = lax.axis_index("sc") % 2 == 0
    close = [(i, i ^ 1) for i in range(size)]
    far = [(i, i + 1) for i in range(1, size - 1, 2)]
    far = far + [(j, i) for i, j in far]
    far = lax.ppermute(jnp.where(even, h[:1], h[-1:]), "sc", far)
    close = lax.ppermute(jnp.where(even, h[-1:], h[:1]), "sc", close)
    return close, far


def over_sections(x):
    return lax.all_to_all(x, "section", split_axis=0, concat_axis=0, tiled=True)


def from_partner(x, bit):
    code = [z ^ (z >> 1) for z in range(lax.axis_size("sc") // 4)]

    def partner(i):
        return i ^ bit if bit < 4 else code.index(code[i // 4] ^ (bit // 4)) * 4 + i % 4

    return lax.ppermute(x, "sc", [(i, partner(i)) for i in range(lax.axis_size("sc"))])


def kernel(body, shapes, in_specs, name, scratch=(), out_specs=None, aliases=None, flops=0, moved=0):
    out = pl.pallas_call(
        body,
        out_shape=[jax.ShapeDtypeStruct(shape, F32) for shape in shapes],
        in_specs=in_specs,
        out_specs=out_specs or [VMEM] * len(shapes),
        scratch_shapes=list(scratch),
        input_output_aliases=aliases or {},
        compiler_params=PARAMS,
        cost_estimate=pl.CostEstimate(flops=flops, bytes_accessed=moved, transcendentals=0),
        name=name,
    )
    return lambda *args: out(*args) if len(shapes) > 1 else out(*args)[0]


def local(observed_vector, propagation_matrix, noise_var, sliced_constellation, detection_sequence):
    h = propagation_matrix.reshape(128, 8, 128)
    noise = noise_var.reshape(1, 128)
    labels = sliced_constellation.transpose(1, 2, 0).reshape(112, 128)
    y = observed_vector.transpose(1, 0, 2)
    big = (8, 128, 128)
    close, far = halo(h)
    rows = (8, 144, 128)
    tile = (8, 128)
    near, aux = kernel(inner_kernel, [rows, tile], [SMEM] + [VMEM] * 3, "inner", flops=10**6, moved=2 * 10**6)(
        detection_sequence, h, labels, noise
    )
    scratch = [pltpu.VMEM((2, 144, 128), F32), pltpu.SemaphoreType.DMA((3,))]
    gathered = over_sections(kernel(edge_kernel, [rows], [VMEM] * 3, "edge", scratch, [ANY])(near, close, far))
    scratch = [pltpu.VMEM(big, F32)]
    gain = kernel(gain_kernel, [tile], [VMEM] * 4, "gain", scratch, flops=10**6, moved=10**6)(near, close, far, aux)
    gain = gain + from_partner(gain, 16)
    gain = kernel(add_kernel, [tile], [VMEM, VMEM, ANY], "add")(gain, from_partner(gain, 4), gathered)
    scratch = [pltpu.VMEM(big, F32), pltpu.VMEM(big, F32)]
    tiles, filters, symbols = kernel(
        filter_kernel, [big, big, (512, 128)], [VMEM, VMEM], "filters", scratch, flops=10**8, moved=4 * 10**6
    )(gathered.reshape(1152, 128), aux)
    scratch = [pltpu.VMEM((16, 16, 128), F32), pltpu.VMEM((256, 128), F32), pltpu.VMEM((256, 128), F32)]
    scratch += [pltpu.VMEM((16, 80, 128), F32), pltpu.SemaphoreType.DMA]
    estimates = kernel(cancel_kernel, [(256, 128)], [VMEM, VMEM, VMEM, ANY], "cancel", scratch, flops=10**8, moved=4 * 10**6)(
        tiles, filters, symbols, y
    )
    estimates, gain = kernel(pack_kernel, [(256, 128), tile], [VMEM] * 3, "pack")(estimates, gain, from_partner(gain, 1))
    estimates = over_sections(estimates.reshape(8, 2, 16, 128))
    gain = kernel(add_kernel, [tile], [VMEM, VMEM, ANY], "add", flops=10**10, moved=10**8)(gain, from_partner(gain, 2), aux)
    gain = gain + from_partner(gain, 8)
    count = float(128 * lax.axis_size("sc"))
    body = lambda *refs: finish_kernel(count, *refs)
    out = kernel(body, [(14, 16, 128)], [VMEM] * 2, "finish", [pltpu.VMEM((14, 16, 128), F32), pltpu.SemaphoreType.DMA((2,))], [ANY])(estimates, gain)
    return out.transpose(2, 0, 1)


def solution(mesh):
    in_specs = (
        P("sc", None, None),
        P("sc", "section", None, None),
        P("sc"),
        P("sc", None, "section"),
        P(),
    )
    out_specs = P("sc", None, "section")
    return jax.shard_map(local, mesh=mesh, in_specs=in_specs, out_specs=out_specs, check_vma=False)
```
